32 devices in a mesh: groups: 2 (over y), row: 4 (over x, core), col: 4 (over z).
Axes of the slice: x: 2, y: 2, z: 4, core: 2. Of those that a mesh axis runs over, the one named last changes fastest.
Arguments:
- upper: bfloat16 [128, 8, 128, 128], P(('groups', 'row', 'col')), parts along dimension 0, as said below
- present: int32 [128, 8], P(('groups', 'row', 'col')), parts along dimension 0, may hold values from 0 to 1, as said below
Outputs:
- purified: bfloat16 [128, 8, 128, 128], P(('groups', 'row', 'col')), parts along dimension 0
The draws below stay inside these ranges and needn't reach their ends.
There are 2 independent parts, one for each index of `groups`. The reference program is written for one: setup_inputs(seed, part) draws one part's arguments, and reference() takes and returns one part's arrays. A program takes and returns all parts, laid end to end along the dimension named above; each array names one. Nothing has to cross between parts.
Inputs may be any that keep to these rules, and one draw needn't show every extreme that they name: upper[i, 0] is a symmetric block for every i. present[i, 0] is 1 for every i.
All inputs are finite; a program needn't handle non-finite values.
Results may differ from the reference program's by a relative error of at most 0.024.
Values may be sent and summed in bfloat16 or wider, within the bound.
No kernel may reach another device: no remote copies, remote signals or barrier semaphores. Data moves between devices by JAX's collectives and lax.ppermute only.
A program may use at most 512 MiB of HBM per device.

```python
import math
import jax
import jax.numpy as jnp

BLOCK = 128
BAND = 7
BLOCK_ROWS = 64


def draw_upper(key, part):
    key = jax.random.fold_in(key, 7)
    first_key = jax.random.fold_in(key, 0)
    shape = (BLOCK_ROWS, BAND + 1, BLOCK, BLOCK)
    base = jax.random.normal(first_key, shape, jnp.float32)
    sigma = 1.0 / math.sqrt(BLOCK * (2 * BAND + 1))
    rows_index = jax.lax.broadcasted_iota(jnp.int32, (BLOCK, BLOCK), 0)
    cols_index = jax.lax.broadcasted_iota(jnp.int32, (BLOCK, BLOCK), 1)
    identity = (rows_index == cols_index).astype(jnp.float32)
    diagonal = 0.5 * identity + 0.5 * sigma * (base[:, 0] + jnp.swapaxes(base[:, 0], 1, 2))
    others = sigma * base[:, 1:]
    return jnp.concatenate([diagonal[:, None], others], axis=1).astype(jnp.bfloat16)


def draw_present(key, part):
    key = jax.random.fold_in(key, 9)
    first_key, second_key = jax.random.split(key)
    levels = jax.random.randint(first_key, (BLOCK_ROWS, 1), 30, 96)
    rolls = jax.random.randint(second_key, (BLOCK_ROWS, BAND + 1), 0, 100)
    offsets = jax.lax.broadcasted_iota(jnp.int32, (BLOCK_ROWS, BAND + 1), 1)
    return jnp.where(offsets == 0, 1, (rolls < levels).astype(jnp.int32)).astype(jnp.int32)


def setup_inputs(seed: int = 0, part: int = 0) -> dict:
    key_list = jax.random.split(jax.random.key(seed), 3)
    part_splits = jax.random.split(jax.random.fold_in(key_list[2], part), 3)
    upper = draw_upper(jax.random.fold_in(jax.random.fold_in(key_list[2], part), 71), part)
    present = draw_present(jax.random.fold_in(jax.random.fold_in(key_list[2], part), 71), part)
    return dict(upper=upper, present=present)


def band_blocks(stored, offset):
    if offset >= 0:
        return stored[:, offset]
    rolled = jnp.roll(stored[:, -offset], -offset, axis=0)
    return jnp.swapaxes(rolled, 1, 2)


def band_square(left, right):
    width = left.shape[1] - 1
    results = []
    for offset in range(width + 1):
        running = jnp.zeros(left.shape[:1] + left.shape[2:], jnp.float32)
        for middle in range(offset - width, width + 1):
            first = band_blocks(left, middle).astype(jnp.float32)
            second = jnp.roll(band_blocks(right, offset - middle), -middle, axis=0).astype(jnp.float32)
            running = running + jnp.einsum("nab,nbc->nac", first, second)
        results.append(running)
    return jnp.stack(results, axis=1)


def reference(upper, present):
    weights = present.astype(jnp.float32)[:, :, None, None]
    masked = upper * present.astype(jnp.bfloat16)[:, :, None, None]
    square = (band_square(masked, masked) * weights).astype(jnp.bfloat16)
    cube = band_square(masked, square) * weights
    return (3.0 * square.astype(jnp.float32) - 2.0 * cube).astype(jnp.bfloat16)
```

```python
import functools

import jax
import jax.numpy as jnp
from jax import lax
from jax.experimental import pallas as pl
from jax.experimental.pallas import tpu as pltpu
from jax.sharding import PartitionSpec as P

B = 128
NT = (((1,), (1,)), ((), ()))
NN = (((1,), (0,)), ((), ()))


def blk(a, n=1):
    return pl.ds(a * B, n * B)


def kernel(z_count, place, present, own, fw1, bw1, fw2, bw2, ends, cross, out, x_ref, y_ref):
    zero = jnp.zeros((B, B), jnp.bfloat16)
    for c in range(1, 9):
        x_ref[blk(0), blk(c)] = zero
    for c in range(11, 27):
        x_ref[blk(19), blk(c)] = zero
    for a in range(1, 19):
        if a % 2 == 0:
            x_ref[blk(a), blk(a + 8)] = zero
        elif a >= 9:
            x_ref[blk(a), blk(a - 8)] = zero

    def put(ref, first, a, count):
        for r in range(count):
            for k in range(8):
                u = ref[first + r, k]
                x_ref[blk(a + r), blk(a + r + k)] = u
                if 0 < k <= 18 - a - r:
                    x_ref[blk(a + r + k), blk(a + r)] = u.T

    z = place[0]
    put(own, 0, 8, 4)
    for at_end, ref, end_ref, first, end_first, a, count in (
        (z == 0, fw1, ends, 0, 0, 4, 4),
        (z == z_count - 1, bw1, ends, 0, 0, 12, 4),
        (z <= 1, fw2, cross, 1, 0, 1, 3),
        (z >= z_count - 2, bw2, cross, 0, 0, 16, 3),
    ):
        pl.when(at_end)(functools.partial(put, end_ref, end_first, a, count))
        pl.when(jnp.logical_not(at_end))(functools.partial(put, ref, first, a, count))

    for L in range(4, 10):
        for J in range(L - 4, L + 1):
            k0 = 2 * L - 7
            n = 2 * J + 9 - k0
            s = lax.dot_general(
                x_ref[blk(2 * J, 2), blk(k0, n)],
                x_ref[blk(2 * L, 2), blk(k0, n)],
                NT,
                preferred_element_type=jnp.float32,
            )
            for dj in range(2):
                for dl in range(2):
                    j, l = 2 * J + dj, 2 * L + dl
                    off = abs(l - j)
                    if off > 7 or j in (0, 19) or l in (0, 19):
                        y_ref[blk(j), blk(l - 8)] = zero
                    else:
                        w = present[min(j, l) * 8 + off].astype(jnp.float32)
                        y_ref[blk(j), blk(l - 8)] = (
                            s[dj * B : (dj + 1) * B, dl * B : (dl + 1) * B] * w
                        ).astype(jnp.bfloat16)
    for I in (4, 5):
        for L in range(I, I + 5):
            k0 = 2 * L - 7
            n = min(2 * L, 2 * I + 8) - k0 + 1
            c = lax.dot_general(
                x_ref[blk(2 * I, 2), blk(k0, n)],
                y_ref[blk(k0, n), blk(2 * L - 8, 2)],
                NN,
                preferred_element_type=jnp.float32,
            )
            n = 2 * I + 8 - 2 * L
            if n > 0:
                c += lax.dot_general(
                    x_ref[blk(2 * I, 2), blk(2 * L + 1, n)],
                    y_ref[blk(2 * L, 2), blk(2 * L - 7, n)],
                    NT,
                    preferred_element_type=jnp.float32,
                )
            for di in range(2):
                for dl in range(2):
                    i, l = 2 * I + di, 2 * L + dl
                    off = l - i
                    if 0 <= off <= 7:
                        w = present[i * 8 + off].astype(jnp.float32)
                        sq = y_ref[blk(i), blk(l - 8)].astype(jnp.float32)
                        cube = w * c[di * B : (di + 1) * B, dl * B : (dl + 1) * B]
                        out[i - 8, off] = (3.0 * sq - 2.0 * cube).astype(jnp.bfloat16)


def compute(z_count, place, present, *rows):
    smem = pl.BlockSpec(memory_space=pltpu.SMEM)
    vmem = pl.BlockSpec(memory_space=pltpu.VMEM)
    return pl.pallas_call(
        functools.partial(kernel, z_count),
        out_shape=jax.ShapeDtypeStruct(rows[0].shape, jnp.bfloat16),
        in_specs=[smem, smem] + [vmem] * len(rows),
        out_specs=vmem,
        scratch_shapes=[
            pltpu.VMEM((20 * B, 28 * B), jnp.bfloat16),
            pltpu.VMEM((20 * B, 12 * B), jnp.bfloat16),
        ],
        compiler_params=pltpu.CompilerParams(vmem_limit_bytes=56 * 1024 * 1024),
    )(place, present, *rows)


def per_device(upper, present):
    s_count, z_count = lax.axis_size("row"), lax.axis_size("col")
    s, z = lax.axis_index("row"), lax.axis_index("col")
    rows, wide = present.shape
    total = rows * s_count * z_count
    masked = upper * present.astype(jnp.bfloat16)[:, :, None, None]

    def step(block, d, pairs=None):
        pairs = pairs or [(i, i + d) for i in range(z_count) if 0 <= i + d < z_count]
        return lax.ppermute(block, "col", pairs)

    def hop(block, route):
        pairs = [
            (i * z_count + a, (i + d) % s_count * z_count + b)
            for i in range(s_count)
            for a, d, b in route
        ]
        return lax.ppermute(block, ("row", "col"), pairs)

    fw1, bw1 = step(masked, 1), step(masked, -1)
    last = z_count - 1
    ends = hop(masked, [(last, 1, 0), (0, -1, last)])
    fw2, bw2 = step(fw1, 1), step(bw1, -1)
    if z_count == 4:
        route = [(0, 1, 0), (1, 1, 1), (2, -1, 2), (3, -1, 3)]
        cross = hop(jnp.where(z < 2, bw2[1:], fw2[:3]), route)
    else:
        route = [(last - 1, 1, 0), (last, 1, 1), (0, -1, last - 1), (1, -1, last)]
        cross = hop(jnp.where(z < 2, masked[:3], masked[1:]), route)
    everyone = lax.all_gather(present, ("row", "col"), tiled=True)
    first = (s * z_count + z) * rows - 8
    window = (first + jnp.arange(20)) % total
    near = jnp.take(everyone, window, axis=0).reshape(-1)
    return compute(z_count, z.reshape(1), near, masked, fw1, bw1, fw2, bw2, ends, cross)


def solution(mesh):
    return jax.shard_map(
        per_device,
        mesh=mesh,
        in_specs=(P(("groups", "row", "col"), None, None, None), P(("groups", "row", "col"), None)),
        out_specs=P(("groups", "row", "col"), None, None, None),
        check_vma=False,
    )
```

```python
import functools

import jax
import jax.numpy as jnp
from jax import lax
from jax.experimental import pallas as pl
from jax.experimental.pallas import tpu as pltpu
from jax.sharding import PartitionSpec as P

B = 128
NT = (((1,), (1,)), ((), ()))
NN = (((1,), (0,)), ((), ()))


def blk(a, n=1):
    return pl.ds(a * B, n * B)


def kernel(z_count, place, own, fw1, bw1, fw2, bw2, ends, cross, out, x_ref, y_ref, w_ref):
    zero = jnp.zeros((B, B), jnp.bfloat16)
    blk8 = pl.ds(8 * B, 16)
    for c in range(1, 9):
        x_ref[blk(0), blk(c)] = zero
    for c in range(11, 27):
        x_ref[blk(19), blk(c)] = zero
    for a in range(1, 19):
        if a % 2 == 0:
            x_ref[blk(a), blk(a + 8)] = zero
        elif a >= 9:
            x_ref[blk(a), blk(a - 8)] = zero

    def put(ref, first, a, count):
        for r in range(count):
            w_ref[a + r] = ref[first + r, blk8].astype(jnp.float32)
            for k in range(8):
                u = ref[first + r, blk(k)]
                x_ref[blk(a + r), blk(a + r + k)] = u
                if 0 < k <= 18 - a - r:
                    x_ref[blk(a + r + k), blk(a + r)] = u.T

    z = place[0]
    put(own, 0, 8, 4)
    for at_end, ref, end_ref, first, end_first, a, count in (
        (z == 0, fw1, ends, 0, 0, 4, 4),
        (z == z_count - 1, bw1, ends, 0, 0, 12, 4),
        (z <= 1, fw2, cross, 1, 0, 1, 3),
        (z >= z_count - 2, bw2, cross, 0, 0, 16, 3),
    ):
        pl.when(at_end)(functools.partial(put, end_ref, end_first, a, count))
        pl.when(jnp.logical_not(at_end))(functools.partial(put, ref, first, a, count))

    for L in range(4, 10):
        for J in range(L - 4, L + 1):
            k0 = 2 * L - 7
            n = 2 * J + 9 - k0
            s = lax.dot_general(
                x_ref[blk(2 * J, 2), blk(k0, n)],
                x_ref[blk(2 * L, 2), blk(k0, n)],
                NT,
                preferred_element_type=jnp.float32,
            )
            for dj in range(2):
                for dl in range(2):
                    j, l = 2 * J + dj, 2 * L + dl
                    off = abs(l - j)
                    if off > 7 or j in (0, 19) or l in (0, 19):
                        y_ref[blk(j), blk(l - 8)] = zero
                    else:
                        w = w_ref[min(j, l), pl.ds(off, 1)]
                        y_ref[blk(j), blk(l - 8)] = (
                            s[dj * B : (dj + 1) * B, dl * B : (dl + 1) * B] * w
                        ).astype(jnp.bfloat16)
    for I in (4, 5):
        for L in range(I, I + 5):
            k0 = 2 * L - 7
            n = min(2 * L, 2 * I + 8) - k0 + 1
            c = lax.dot_general(
                x_ref[blk(2 * I, 2), blk(k0, n)],
                y_ref[blk(k0, n), blk(2 * L - 8, 2)],
                NN,
                preferred_element_type=jnp.float32,
            )
            n = 2 * I + 8 - 2 * L
            if n > 0:
                c += lax.dot_general(
                    x_ref[blk(2 * I, 2), blk(2 * L + 1, n)],
                    y_ref[blk(2 * L, 2), blk(2 * L - 7, n)],
                    NT,
                    preferred_element_type=jnp.float32,
                )
            for di in range(2):
                for dl in range(2):
                    i, l = 2 * I + di, 2 * L + dl
                    off = l - i
                    if 0 <= off <= 7:
                        w = w_ref[i, pl.ds(off, 1)]
                        sq = y_ref[blk(i), blk(l - 8)].astype(jnp.float32)
                        cube = w * c[di * B : (di + 1) * B, dl * B : (dl + 1) * B]
                        out[i - 8, off] = (3.0 * sq - 2.0 * cube).astype(jnp.bfloat16)


def compute(z_count, place, *rows):
    smem = pl.BlockSpec(memory_space=pltpu.SMEM)
    vmem = pl.BlockSpec(memory_space=pltpu.VMEM)
    return pl.pallas_call(
        functools.partial(kernel, z_count),
        out_shape=jax.ShapeDtypeStruct((4, 8, B, B), jnp.bfloat16),
        in_specs=[smem] + [vmem] * len(rows),
        out_specs=vmem,
        scratch_shapes=[
            pltpu.VMEM((20 * B, 28 * B), jnp.bfloat16),
            pltpu.VMEM((20 * B, 12 * B), jnp.bfloat16),
            pltpu.VMEM((20, 16, B), jnp.float32),
        ],
        compiler_params=pltpu.CompilerParams(vmem_limit_bytes=56 * 1024 * 1024),
    )(place, *rows)


def per_device(upper, present):
    s_count, z_count = lax.axis_size("row"), lax.axis_size("col")
    z = lax.axis_index("col")
    rows, wide = present.shape
    weights = present.astype(jnp.bfloat16)[:, :, None, None]
    blocks = (upper * weights).reshape(rows, wide * B, B)
    pattern = jnp.broadcast_to(weights[:, :, 0], (rows, wide, B))
    masked = jnp.concatenate([blocks, pattern, pattern], axis=1)

    def step(block, d, pairs=None):
        pairs = pairs or [(i, i + d) for i in range(z_count) if 0 <= i + d < z_count]
        return lax.ppermute(block, "col", pairs)

    def hop(block, route):
        pairs = [
            (i * z_count + a, (i + d) % s_count * z_count + b)
            for i in range(s_count)
            for a, d, b in route
        ]
        return lax.ppermute(block, ("row", "col"), pairs)

    fw1, bw1 = step(masked, 1), step(masked, -1)
    last = z_count - 1
    ends = hop(masked, [(last, 1, 0), (0, -1, last)])
    fw2, bw2 = step(fw1, 1), step(bw1, -1)
    if z_count == 4:
        route = [(0, 1, 0), (1, 1, 1), (2, -1, 2), (3, -1, 3)]
        cross = hop(jnp.where(z < 2, bw2[1:], fw2[:3]), route)
    else:
        route = [(last - 1, 1, 0), (last, 1, 1), (0, -1, last - 1), (1, -1, last)]
        cross = hop(jnp.where(z < 2, masked[:3], masked[1:]), route)
    return compute(z_count, z.reshape(1), masked, fw1, bw1, fw2, bw2, ends, cross)


def solution(mesh):
    return jax.shard_map(
        per_device,
        mesh=mesh,
        in_specs=(P(("groups", "row", "col"), None, None, None), P(("groups", "row", "col"), None)),
        out_specs=P(("groups", "row", "col"), None, None, None),
        check_vma=False,
    )
```

```python
import functools

import jax
import jax.numpy as jnp
from jax import lax
from jax.experimental import pallas as pl
from jax.experimental.pallas import tpu as pltpu
from jax.sharding import PartitionSpec as P

B = 128
NT = (((1,), (1,)), ((), ()))
NN = (((1,), (0,)), ((), ()))


def blk(a, n=1):
    return pl.ds(a * B, n * B)


def kernel(z_count, place, own, fw1a, fw1b, bw1a, bw1b, fw2a, fw2b, bw2a, bw2b, endsa, endsb, cross, out, x_ref, y_ref, w_ref):
    zero = jnp.zeros((B, B), jnp.bfloat16)
    blk8 = pl.ds(8 * B, 16)
    for c in range(1, 9):
        x_ref[blk(0), blk(c)] = zero
    for c in range(11, 27):
        x_ref[blk(19), blk(c)] = zero
    for a in range(1, 19):
        if a % 2 == 0:
            x_ref[blk(a), blk(a + 8)] = zero
        elif a >= 9:
            x_ref[blk(a), blk(a - 8)] = zero

    def put(ref, first, a, count):
        for r in range(count):
            w_ref[a + r] = ref[first + r, blk8].astype(jnp.float32)
            for k in range(8):
                u = ref[first + r, blk(k)]
                x_ref[blk(a + r), blk(a + r + k)] = u
                if 0 < k <= 18 - a - r:
                    x_ref[blk(a + r + k), blk(a + r)] = u.T

    z = place[0]
    put(own, 0, 8, 4)
    for at_end, ref, end_ref, first, end_first, a, count in (
        (z == 0, fw1a, endsa, 0, 0, 4, 2),
        (z == 0, fw1b, endsb, 0, 0, 6, 2),
        (z == z_count - 1, bw1a, endsa, 0, 0, 12, 2),
        (z == z_count - 1, bw1b, endsb, 0, 0, 14, 2),
        (z <= 1, fw2a, cross, 1, 0, 1, 1),
        (z <= 1, fw2b, cross, 0, 1, 2, 2),
        (z >= z_count - 2, bw2a, cross, 0, 0, 16, 2),
        (z >= z_count - 2, bw2b, cross, 0, 2, 18, 1),
    ):
        pl.when(at_end)(functools.partial(put, end_ref, end_first, a, count))
        pl.when(jnp.logical_not(at_end))(functools.partial(put, ref, first, a, count))

    for L in range(4, 10):
        for J in range(L - 4, L + 1):
            k0 = 2 * L - 7
            n = 2 * J + 9 - k0
            s = lax.dot_general(
                x_ref[blk(2 * J, 2), blk(k0, n)],
                x_ref[blk(2 * L, 2), blk(k0, n)],
                NT,
                preferred_element_type=jnp.float32,
            )
            for dj in range(2):
                for dl in range(2):
                    j, l = 2 * J + dj, 2 * L + dl
                    off = abs(l - j)
                    if off > 7 or j in (0, 19) or l in (0, 19):
                        y_ref[blk(j), blk(l - 8)] = zero
                    else:
                        w = w_ref[min(j, l), pl.ds(off, 1)]
                        y_ref[blk(j), blk(l - 8)] = (
                            s[dj * B : (dj + 1) * B, dl * B : (dl + 1) * B] * w
                        ).astype(jnp.bfloat16)
    for I in (4, 5):
        for L in range(I, I + 5):
            k0 = 2 * L - 7
            n = min(2 * L, 2 * I + 8) - k0 + 1
            c = lax.dot_general(
                x_ref[blk(2 * I, 2), blk(k0, n)],
                y_ref[blk(k0, n), blk(2 * L - 8, 2)],
                NN,
                preferred_element_type=jnp.float32,
            )
            n = 2 * I + 8 - 2 * L
            if n > 0:
                c += lax.dot_general(
                    x_ref[blk(2 * I, 2), blk(2 * L + 1, n)],
                    y_ref[blk(2 * L, 2), blk(2 * L - 7, n)],
                    NT,
                    preferred_element_type=jnp.float32,
                )
            for di in range(2):
                for dl in range(2):
                    i, l = 2 * I + di, 2 * L + dl
                    off = l - i
                    if 0 <= off <= 7:
                        w = w_ref[i, pl.ds(off, 1)]
                        sq = y_ref[blk(i), blk(l - 8)].astype(jnp.float32)
                        cube = w * c[di * B : (di + 1) * B, dl * B : (dl + 1) * B]
                        out[i - 8, off] = (3.0 * sq - 2.0 * cube).astype(jnp.bfloat16)


def compute(z_count, place, *rows):
    smem = pl.BlockSpec(memory_space=pltpu.SMEM)
    vmem = pl.BlockSpec(memory_space=pltpu.VMEM)
    return pl.pallas_call(
        functools.partial(kernel, z_count),
        out_shape=jax.ShapeDtypeStruct((4, 8, B, B), jnp.bfloat16),
        in_specs=[smem] + [vmem] * len(rows),
        out_specs=vmem,
        scratch_shapes=[
            pltpu.VMEM((20 * B, 28 * B), jnp.bfloat16),
            pltpu.VMEM((20 * B, 12 * B), jnp.bfloat16),
            pltpu.VMEM((20, 16, B), jnp.float32),
        ],
        compiler_params=pltpu.CompilerParams(vmem_limit_bytes=56 * 1024 * 1024),
    )(place, *rows)


def per_device(upper, present):
    s_count, z_count = lax.axis_size("row"), lax.axis_size("col")
    z = lax.axis_index("col")
    rows, wide = present.shape
    weights = present.astype(jnp.bfloat16)[:, :, None, None]
    blocks = (upper * weights).reshape(rows, wide * B, B)
    pattern = jnp.broadcast_to(weights[:, :, 0], (rows, wide, B))
    masked = jnp.concatenate([blocks, pattern, pattern], axis=1)

    def step(block, d, pairs=None):
        pairs = pairs or [(i, i + d) for i in range(z_count) if 0 <= i + d < z_count]
        return lax.ppermute(block, "col", pairs)

    def hop(block, route):
        pairs = [
            (i * z_count + a, (i + d) % s_count * z_count + b)
            for i in range(s_count)
            for a, d, b in route
        ]
        return lax.ppermute(block, ("row", "col"), pairs)

    last = z_count - 1
    inner = range(1, last)
    parts = [masked[: rows // 2], masked[rows // 2 :]]
    fw1 = [step(part, 1) for part in parts]
    bw1 = [step(part, -1) for part in parts]
    fw2 = [step(part, 1, [(i, i + 1) for i in inner]) for part in fw1]
    bw2 = [step(part, -1, [(i, i - 1) for i in inner]) for part in bw1]
    if z_count == 4:
        ends = [
            hop(jnp.where(z < 2, down, up), [(1, 1, 0), (2, -1, 3)]) for down, up in zip(bw2, fw2)
        ]
        route = [(0, 1, 0), (1, 1, 1), (2, -1, 2), (3, -1, 3)]
        below = jnp.concatenate([bw2[0][1:], bw2[1]])
        above = jnp.concatenate([fw2[0], fw2[1][:1]])
        cross = hop(jnp.where(z < 2, below, above), route)
    else:
        ends = [hop(part, [(last, 1, 0), (0, -1, last)]) for part in parts]
        route = [(last - 1, 1, 0), (last, 1, 1), (0, -1, last - 1), (1, -1, last)]
        cross = hop(jnp.where(z < 2, masked[:3], masked[1:]), route)
    return compute(z_count, z.reshape(1), masked, *fw1, *bw1, *fw2, *bw2, *ends, cross)


def solution(mesh):
    return jax.shard_map(
        per_device,
        mesh=mesh,
        in_specs=(P(("groups", "row", "col"), None, None, None), P(("groups", "row", "col"), None)),
        out_specs=P(("groups", "row", "col"), None, None, None),
        check_vma=False,
    )
```

```python
import functools

import jax
import jax.numpy as jnp
from jax import lax
from jax.experimental import pallas as pl
from jax.experimental.pallas import tpu as pltpu
from jax.sharding import PartitionSpec as P

B = 128
NT = (((1,), (1,)), ((), ()))
NN = (((1,), (0,)), ((), ()))


def blk(a, n=1):
    return pl.ds(a * B, n * B)


def put(x_ref, w_ref, ref, first, a, count):
    for r in range(count):
        w_ref[a + r] = ref[first + r, pl.ds(8 * B, 16)].astype(jnp.float32)
        for k in range(8):
            u = ref[first + r, blk(k)]
            set_x(x_ref, a + r, a + r + k, u)
            if 0 < k <= 18 - a - r:
                set_x(x_ref, a + r + k, a + r, u.T)


def set_x(x_ref, a, b, value):
    x_ref[a // 2, blk(a % 2), blk(b - a // 2 * 2 + 7)] = value


def square(x_ref, y_ref, w_ref, pairs):
    zero = jnp.zeros((B, B), jnp.bfloat16)
    for L in pairs:
        for J in range(L - 4, L + 1):
            d = L - J
            s = lax.dot_general(
                x_ref[J, :, blk(2 * d, 16 - 2 * d)],
                x_ref[L, :, blk(0, 16 - 2 * d)],
                NT,
                preferred_element_type=jnp.float32,
            )
            for dj in range(2):
                for dl in range(2):
                    j, l = 2 * J + dj, 2 * L + dl
                    off = abs(l - j)
                    if off > 7 or j in (0, 19) or l in (0, 19):
                        y_ref[blk(j), blk(l - 8)] = zero
                    else:
                        w = w_ref[min(j, l), pl.ds(off, 1)]
                        y_ref[blk(j), blk(l - 8)] = (
                            s[dj * B : (dj + 1) * B, dl * B : (dl + 1) * B] * w
                        ).astype(jnp.bfloat16)


def purify(x_ref, y_ref, w_ref, out):
    for I in (4, 5):
        for L in range(I, I + 5):
            d = L - I
            k0 = 2 * L - 7
            n = min(2 * L, 2 * I + 8) - k0 + 1
            c = lax.dot_general(
                x_ref[I, :, blk(2 * d, n)],
                y_ref[blk(k0, n), blk(2 * L - 8, 2)],
                NN,
                preferred_element_type=jnp.float32,
            )
            if d < 4:
                n = 8 - 2 * d
                c += lax.dot_general(
                    x_ref[I, :, blk(2 * d + 8, n)],
                    y_ref[blk(2 * L, 2), blk(2 * L - 7, n)],
                    NT,
                    preferred_element_type=jnp.float32,
                )
            for di in range(2):
                for dl in range(2):
                    i, l = 2 * I + di, 2 * L + dl
                    off = l - i
                    if 0 <= off <= 7:
                        w = w_ref[i, pl.ds(off, 1)]
                        sq = y_ref[blk(i), blk(l - 8)].astype(jnp.float32)
                        cube = w * c[di * B : (di + 1) * B, dl * B : (dl + 1) * B]
                        out[i - 8, off] = (3.0 * sq - 2.0 * cube).astype(jnp.bfloat16)


def first_kernel(z_count, place, own, fw1a, fw1b, bw1a, bw1b, fw2a, fw2b, bw2a, bw2b, ends, x_ref, y_ref, w_ref):
    zero = jnp.zeros((B, B), jnp.bfloat16)
    for c in range(16):
        set_x(x_ref, 0, c - 7, zero)
        set_x(x_ref, 19, c + 11, zero)
    for a in range(1, 19):
        set_x(x_ref, a, a + 8 if a % 2 == 0 else a - 8, zero)
    z = place[0]
    last = z_count - 1
    take = functools.partial(put, x_ref, w_ref)
    take(own, 0, 8, 4)
    for here, ref, first, a, count in (
        (z == 0, ends, 0, 6, 2),
        (z > 0, fw1b, 0, 6, 2),
        (z > 0, fw1a, 0, 4, 2),
        (z == last, ends, 0, 12, 2),
        (z < last, bw1a, 0, 12, 2),
        (z < last, bw1b, 0, 14, 2),
        (z > 1, fw2a, 1, 1, 1),
        (z > 1, fw2b, 0, 2, 2),
        (z < last - 1, bw2a, 0, 16, 2),
        (z < last - 1, bw2b, 0, 18, 1),
    ):
        pl.when(here)(functools.partial(take, ref, first, a, count))
    low = z < z_count // 2
    pl.when(low)(functools.partial(square, x_ref, y_ref, w_ref, (7, 8, 9)))
    pl.when(jnp.logical_not(low))(functools.partial(square, x_ref, y_ref, w_ref, (4, 5, 6)))


def second_kernel(z_count, place, x_in, y_in, w_in, ends, cross, out, x_ref, y_ref, w_ref):
    z = place[0]
    last = z_count - 1
    take = functools.partial(put, x_ref, w_ref)
    for here, ref, first, a, count in (
        (z == 0, ends, 0, 4, 2),
        (z == last, ends, 0, 14, 2),
        (z <= 1, cross, 0, 1, 3),
        (z >= last - 1, cross, 0, 16, 3),
    ):
        pl.when(here)(functools.partial(take, ref, first, a, count))
    low = z < z_count // 2
    pl.when(low)(functools.partial(square, x_ref, y_ref, w_ref, (4, 5, 6)))
    pl.when(jnp.logical_not(low))(functools.partial(square, x_ref, y_ref, w_ref, (7, 8, 9)))
    purify(x_ref, y_ref, w_ref, out)


SMEM = pl.BlockSpec(memory_space=pltpu.SMEM)
VMEM = pl.BlockSpec(memory_space=pltpu.VMEM)
KEPT = [
    pltpu.VMEM((10, 2 * B, 16 * B), jnp.bfloat16),
    pltpu.VMEM((20 * B, 12 * B), jnp.bfloat16),
    pltpu.VMEM((20, 16, B), jnp.float32),
]


def compute(z_count, place, early, late):
    kept = pl.pallas_call(
        functools.partial(first_kernel, z_count),
        out_shape=KEPT,
        in_specs=[SMEM] + [VMEM] * len(early),
        out_specs=[VMEM] * 3,
        compiler_params=pltpu.CompilerParams(vmem_limit_bytes=24 * 1024 * 1024),
        cost_estimate=pl.CostEstimate(flops=6 * 10**9, bytes_accessed=6 * 10**6, transcendentals=0),
    )(place, *early)
    return pl.pallas_call(
        functools.partial(second_kernel, z_count),
        out_shape=[jax.ShapeDtypeStruct((4, 8, B, B), jnp.bfloat16)] + KEPT,
        in_specs=[SMEM] + [VMEM] * (3 + len(late)),
        out_specs=[VMEM] * 4,
        input_output_aliases={1: 1, 2: 2, 3: 3},
        compiler_params=pltpu.CompilerParams(vmem_limit_bytes=24 * 1024 * 1024),
        cost_estimate=pl.CostEstimate(flops=6 * 10**9, bytes_accessed=4 * 10**6, transcendentals=0),
    )(place, *kept, *late)[0]


def per_device(upper, present):
    s_count, z_count = lax.axis_size("row"), lax.axis_size("col")
    z = lax.axis_index("col")
    rows, wide = present.shape
    weights = present.astype(jnp.bfloat16)[:, :, None, None]
    blocks = (upper * weights).reshape(rows, wide * B, B)
    pattern = jnp.broadcast_to(weights[:, :, 0], (rows, wide, B))
    masked = jnp.concatenate([blocks, pattern, pattern], axis=1)

    def step(block, d, pairs=None):
        pairs = pairs or [(i, i + d) for i in range(z_count) if 0 <= i + d < z_count]
        return lax.ppermute(block, "col", pairs)

    def hop(block, route):
        pairs = [
            (i * z_count + a, (i + d) % s_count * z_count + b)
            for i in range(s_count)
            for a, d, b in route
        ]
        return lax.ppermute(block, ("row", "col"), pairs)

    last = z_count - 1
    inner = range(1, last)
    parts = [masked[: rows // 2], masked[rows // 2 :]]
    fw1 = [step(part, 1) for part in parts]
    bw1 = [step(part, -1) for part in parts]
    fw2 = [step(part, 1, [(i, i + 1) for i in inner]) for part in fw1]
    bw2 = [step(part, -1, [(i, i - 1) for i in inner]) for part in bw1]
    if z_count == 4:
        route = [(1, 1, 0), (2, -1, 3)]
        ends_first = hop(jnp.where(z < 2, bw2[1], fw2[0]), route)
        ends_last = hop(jnp.where(z < 2, bw2[0], fw2[1]), route)
        route = [(0, 1, 0), (1, 1, 1), (2, -1, 2), (3, -1, 3)]
        below = jnp.concatenate([bw2[0][1:], bw2[1]])
        above = jnp.concatenate([fw2[0], fw2[1][:1]])
        cross = hop(jnp.where(z < 2, below, above), route)
    else:
        route = [(last, 1, 0), (0, -1, last)]
        ends_first = hop(jnp.where(z == last, parts[1], parts[0]), route)
        ends_last = hop(jnp.where(z == last, parts[0], parts[1]), route)
        route = [(last - 1, 1, 0), (last, 1, 1), (0, -1, last - 1), (1, -1, last)]
        cross = hop(jnp.where(z < 2, masked[:3], masked[1:]), route)
    early = (masked, *fw1, *bw1, *fw2, *bw2, ends_first)
    return compute(z_count, z.reshape(1), early, (ends_last, cross))


def solution(mesh):
    return jax.shard_map(
        per_device,
        mesh=mesh,
        in_specs=(P(("groups", "row", "col"), None, None, None), P(("groups", "row", "col"), None)),
        out_specs=P(("groups", "row", "col"), None, None, None),
        check_vma=False,
    )
```

```python
import functools

import jax
import jax.numpy as jnp
from jax import lax
from jax.experimental import pallas as pl
from jax.experimental.pallas import tpu as pltpu
from jax.sharding import PartitionSpec as P

B = 128
NT = (((1,), (1,)), ((), ()))
NN = (((1,), (0,)), ((), ()))


def blk(a, n=1):
    return pl.ds(a * B, n * B)


def triangles():
    p = lax.broadcasted_iota(jnp.int32, (B, B), 0)
    q = lax.broadcasted_iota(jnp.int32, (B, B), 1)
    return p, q


def pack(present, upper, _, *outs):
    p, q = triangles()
    right = lax.broadcasted_iota(jnp.int32, (1, B), 1) >= B // 2

    def block(r, k):
        w = present[r, k].astype(jnp.float32)
        return upper[r, k].astype(jnp.float32) * w

    for first, out in zip((0, 2), outs):
        one, two = block(first, 0), block(first + 1, 0)
        out[blk(0)] = jnp.where(p <= q, one, two).astype(jnp.bfloat16)
        for r in range(2):
            for k in range(1, 8):
                out[blk(7 * r + k)] = block(first + r, k).astype(jnp.bfloat16)
        lines = [
            jnp.where(
                right,
                present[first + 1, k].astype(jnp.float32),
                present[first, k].astype(jnp.float32),
            )
            for k in range(8)
        ]
        lines.append(jnp.sum(jnp.where(p == q, two, 0.0), axis=0, keepdims=True))
        lines.append(jnp.zeros((7, B), jnp.float32))
        out[pl.ds(15 * B, 16)] = jnp.concatenate(lines, axis=0).astype(jnp.bfloat16)


def put(x_ref, w_ref, ref, a, rows=(0, 1)):
    p, q = triangles()
    mixed = ref[blk(0)].astype(jnp.float32)
    turned = mixed.T
    tail = ref[pl.ds(15 * B, 16)].astype(jnp.float32)
    for r in rows:
        w_ref[a + r] = jnp.broadcast_to(tail[:8, r * B // 2 : r * B // 2 + 1], (8, B))
        if r == 0:
            diagonal = jnp.where(p <= q, mixed, turned)
        else:
            diagonal = jnp.where(p > q, mixed, jnp.where(p < q, turned, tail[8:9]))
        set_x(x_ref, a + r, a + r, diagonal.astype(jnp.bfloat16))
        for k in range(1, 8):
            u = ref[blk(7 * r + k)]
            set_x(x_ref, a + r, a + r + k, u)
            if k <= 18 - a - r:
                set_x(x_ref, a + r + k, a + r, u.T)


def set_x(x_ref, a, b, value):
    x_ref[a // 2, blk(a % 2), blk(b - a // 2 * 2 + 7)] = value


def square(x_ref, y_ref, w_ref, pairs):
    zero = jnp.zeros((B, B), jnp.bfloat16)
    for L in pairs:
        for J in range(L - 4, L + 1):
            d = L - J
            s = lax.dot_general(
                x_ref[J, :, blk(2 * d, 16 - 2 * d)],
                x_ref[L, :, blk(0, 16 - 2 * d)],
                NT,
                preferred_element_type=jnp.float32,
            )
            for dj in range(2):
                for dl in range(2):
                    j, l = 2 * J + dj, 2 * L + dl
                    off = abs(l - j)
                    if off > 7 or j in (0, 19) or l in (0, 19):
                        y_ref[blk(j), blk(l - 8)] = zero
                    else:
                        w = w_ref[min(j, l), pl.ds(off, 1)]
                        y_ref[blk(j), blk(l - 8)] = (
                            s[dj * B : (dj + 1) * B, dl * B : (dl + 1) * B] * w
                        ).astype(jnp.bfloat16)


def purify(x_ref, y_ref, w_ref, out):
    for I in (4, 5):
        for L in range(I, I + 5):
            d = L - I
            k0 = 2 * L - 7
            n = min(2 * L, 2 * I + 8) - k0 + 1
            c = lax.dot_general(
                x_ref[I, :, blk(2 * d, n)],
                y_ref[blk(k0, n), blk(2 * L - 8, 2)],
                NN,
                preferred_element_type=jnp.float32,
            )
            if d < 4:
                n = 8 - 2 * d
                c += lax.dot_general(
                    x_ref[I, :, blk(2 * d + 8, n)],
                    y_ref[blk(2 * L, 2), blk(2 * L - 7, n)],
                    NT,
                    preferred_element_type=jnp.float32,
                )
            for di in range(2):
                for dl in range(2):
                    i, l = 2 * I + di, 2 * L + dl
                    off = l - i
                    if 0 <= off <= 7:
                        w = w_ref[i, pl.ds(off, 1)]
                        sq = y_ref[blk(i), blk(l - 8)].astype(jnp.float32)
                        cube = w * c[di * B : (di + 1) * B, dl * B : (dl + 1) * B]
                        out[i - 8, off] = (3.0 * sq - 2.0 * cube).astype(jnp.bfloat16)


def first_kernel(z_count, place, owna, ownb, fw1a, fw1b, bw1a, bw1b, fw2a, fw2b, bw2a, bw2b, ends, x_ref, y_ref, w_ref):
    zero = jnp.zeros((B, B), jnp.bfloat16)
    for c in range(16):
        set_x(x_ref, 0, c - 7, zero)
        set_x(x_ref, 19, c + 11, zero)
    for a in range(1, 19):
        set_x(x_ref, a, a + 8 if a % 2 == 0 else a - 8, zero)
    z = place[0]
    last = z_count - 1
    take = functools.partial(put, x_ref, w_ref)
    take(owna, 8)
    take(ownb, 10)
    for here, ref, a, rows in (
        (z == 0, ends, 6, (0, 1)),
        (z > 0, fw1b, 6, (0, 1)),
        (z > 0, fw1a, 4, (0, 1)),
        (z == last, ends, 12, (0, 1)),
        (z < last, bw1a, 12, (0, 1)),
        (z < last, bw1b, 14, (0, 1)),
        (z > 1, fw2a, 0, (1,)),
        (z > 1, fw2b, 2, (0, 1)),
        (z < last - 1, bw2a, 16, (0, 1)),
        (z < last - 1, bw2b, 18, (0,)),
    ):
        pl.when(here)(functools.partial(take, ref, a, rows))
    low = z < z_count // 2
    pl.when(low)(functools.partial(square, x_ref, y_ref, w_ref, (7, 8, 9)))
    pl.when(jnp.logical_not(low))(functools.partial(square, x_ref, y_ref, w_ref, (4, 5, 6)))


def second_kernel(z_count, place, x_in, y_in, w_in, ends, cross_first, cross_last, out, x_ref, y_ref, w_ref):
    z = place[0]
    last = z_count - 1
    take = functools.partial(put, x_ref, w_ref)
    for here, ref, a, rows in (
        (z == 0, ends, 4, (0, 1)),
        (z == last, ends, 14, (0, 1)),
        (z <= 1, cross_first, 2, (0, 1)),
        (z <= 1, cross_last, 0, (1,)),
        (z >= last - 1, cross_first, 16, (0, 1)),
        (z >= last - 1, cross_last, 18, (0,)),
    ):
        pl.when(here)(functools.partial(take, ref, a, rows))
    low = z < z_count // 2
    pl.when(low)(functools.partial(square, x_ref, y_ref, w_ref, (4, 5, 6)))
    pl.when(jnp.logical_not(low))(functools.partial(square, x_ref, y_ref, w_ref, (7, 8, 9)))
    purify(x_ref, y_ref, w_ref, out)


SMEM = pl.BlockSpec(memory_space=pltpu.SMEM)
VMEM = pl.BlockSpec(memory_space=pltpu.VMEM)
KEPT = [
    pltpu.VMEM((10, 2 * B, 16 * B), jnp.bfloat16),
    pltpu.VMEM((20 * B, 12 * B), jnp.bfloat16),
    pltpu.VMEM((20, 8, B), jnp.float32),
]


def compute(z_count, place, early, late):
    kept = pl.pallas_call(
        functools.partial(first_kernel, z_count),
        out_shape=KEPT,
        in_specs=[SMEM] + [VMEM] * len(early),
        out_specs=[VMEM] * 3,
        compiler_params=pltpu.CompilerParams(vmem_limit_bytes=24 * 1024 * 1024),
        cost_estimate=pl.CostEstimate(flops=6 * 10**9, bytes_accessed=6 * 10**6, transcendentals=0),
    )(place, *early)
    return pl.pallas_call(
        functools.partial(second_kernel, z_count),
        out_shape=[jax.ShapeDtypeStruct((4, 8, B, B), jnp.bfloat16)] + KEPT,
        in_specs=[SMEM] + [VMEM] * (3 + len(late)),
        out_specs=[VMEM] * 4,
        input_output_aliases={1: 1, 2: 2, 3: 3},
        compiler_params=pltpu.CompilerParams(vmem_limit_bytes=24 * 1024 * 1024),
        cost_estimate=pl.CostEstimate(flops=6 * 10**9, bytes_accessed=4 * 10**6, transcendentals=0),
    )(place, *kept, *late)[0]


def packed(present, upper, before):
    rows = upper.shape[2]
    pair = jax.ShapeDtypeStruct((15 * rows + 16, rows), jnp.bfloat16)
    return pl.pallas_call(
        pack,
        out_shape=[pair, pair],
        in_specs=[SMEM, VMEM, pl.BlockSpec(memory_space=pl.ANY)],
        out_specs=[VMEM, VMEM],
        compiler_params=pltpu.CompilerParams(vmem_limit_bytes=8 * 1024 * 1024),
    )(present, upper, before)


def per_device(upper, present):
    s_count, z_count = lax.axis_size("row"), lax.axis_size("col")
    z = lax.axis_index("col")
    def step(block, d, pairs=None):
        pairs = pairs or [(i, i + d) for i in range(z_count) if 0 <= i + d < z_count]
        return lax.ppermute(block, "col", pairs)

    def hop(block, route):
        pairs = [
            (i * z_count + a, (i + d) % s_count * z_count + b)
            for i in range(s_count)
            for a, d, b in route
        ]
        return lax.ppermute(block, ("row", "col"), pairs)

    last = z_count - 1
    inner = range(1, last)
    parts = packed(present, upper, present)
    again = packed(present, upper, parts[0])
    fw1 = [step(parts[0], 1), step(again[1], 1)]
    bw1 = [step(again[0], -1), step(parts[1], -1)]
    fw2 = [step(part, 1, [(i, i + 1) for i in inner]) for part in fw1]
    bw2 = [step(part, -1, [(i, i - 1) for i in inner]) for part in bw1]
    if z_count == 4:
        to_end, beside = [(1, 1, 0), (2, -1, 3)], [(0, 1, 0), (1, 1, 1), (2, -1, 2), (3, -1, 3)]
        sooner = jnp.where(z < 2, bw2[1], fw2[0])
        ends_first = hop(sooner, to_end)
        cross_first = hop(sooner, beside)
        down, up = lax.optimization_barrier((bw2[0], fw2[1]))
        later = jnp.where(z < 2, down, up)
        ends_last = hop(later, to_end)
        cross_last = hop(later, beside)
    else:
        route = [(last, 1, 0), (0, -1, last)]
        ends_first = hop(jnp.where(z == last, parts[1], parts[0]), route)
        ends_last = hop(jnp.where(z == last, parts[0], parts[1]), route)
        route = [(last - 1, 1, 0), (last, 1, 1), (0, -1, last - 1), (1, -1, last)]
        cross_first = hop(jnp.where(z < 2, parts[0], parts[1]), route)
        cross_last = hop(jnp.where(z < 2, parts[1], parts[0]), route)
    early = (*parts, *fw1, *bw1, *fw2, *bw2, ends_first)
    return compute(z_count, z.reshape(1), early, (ends_last, cross_first, cross_last))


def solution(mesh):
    return jax.shard_map(
        per_device,
        mesh=mesh,
        in_specs=(P(("groups", "row", "col"), None, None, None), P(("groups", "row", "col"), None)),
        out_specs=P(("groups", "row", "col"), None, None, None),
        check_vma=False,
    )
```

```python
import functools

import jax
import jax.numpy as jnp
from jax import lax
from jax.experimental import pallas as pl
from jax.experimental.pallas import tpu as pltpu
from jax.sharding import PartitionSpec as P

B = 128
NT = (((1,), (1,)), ((), ()))
NN = (((1,), (0,)), ((), ()))

MIXED = 7 * B
TAIL = 8 * B
SECOND = 8 * B + 16
PAIR = 15 * B + 16
ONE = SECOND

LOW = {1: 2, 2: 1, 3: 1, 4: 2, 5: 2, 6: 1, 7: 1}
HIGH = {12: 1, 13: 1, 14: 2, 15: 2, 16: 1, 17: 1, 18: 2}


def blk(a, n=1):
    return pl.ds(a * B, n * B)


def x_stage(late, J, m):
    return max(late.get(min(2 * J, m), 0), late.get(min(2 * J + 1, m), 0))


def square_terms(late, J, L):
    return [
        (m, max(x_stage(late, J, m), x_stage(late, L, m))) for m in range(2 * L - 7, 2 * J + 9)
    ]


def y_stage(late, J, L):
    return max(stage for _, stage in square_terms(late, min(J, L), max(J, L)))


def cube_terms(late, I, L):
    return [
        (j, max(x_stage(late, I, j), y_stage(late, j // 2, L))) for j in range(2 * L - 7, 2 * I + 9)
    ]


def runs(columns):
    found = []
    for m in columns:
        if found and found[-1][0] + found[-1][1] == m:
            found[-1][1] += 1
        else:
            found.append([m, 1])
    return found


def triangles():
    p = lax.broadcasted_iota(jnp.int32, (B, B), 0)
    q = lax.broadcasted_iota(jnp.int32, (B, B), 1)
    return p, q


def pack(present, upper, _, *outs):
    p, q = triangles()
    right = lax.broadcasted_iota(jnp.int32, (1, B), 1) >= B // 2

    def block(r, k):
        w = present[r, k].astype(jnp.float32)
        return upper[r, k].astype(jnp.float32) * w

    for first, out in zip((0, 2), outs):
        one, two = block(first, 0), block(first + 1, 0)
        out[pl.ds(MIXED, B)] = jnp.where(p <= q, one, two).astype(jnp.bfloat16)
        for r in range(2):
            for k in range(1, 8):
                out[pl.ds(SECOND * r + (k - 1) * B, B)] = block(first + r, k).astype(jnp.bfloat16)
        lines = [
            jnp.where(
                right,
                present[first + 1, k].astype(jnp.float32),
                present[first, k].astype(jnp.float32),
            )
            for k in range(8)
        ]
        lines.append(jnp.sum(jnp.where(p == q, two, 0.0), axis=0, keepdims=True))
        lines.append(jnp.zeros((7, B), jnp.float32))
        out[pl.ds(TAIL, 16)] = jnp.concatenate(lines, axis=0).astype(jnp.bfloat16)


def set_x(x_ref, a, b, value):
    x_ref[a // 2, blk(a % 2), blk(b - a // 2 * 2 + 7)] = value


def put(x_ref, w_ref, ref, a, rows=(0, 1), skip=0):
    p, q = triangles()
    mixed = ref[pl.ds(MIXED - skip, B)].astype(jnp.float32)
    turned = mixed.T
    tail = ref[pl.ds(TAIL - skip, 16)].astype(jnp.float32)
    for r in rows:
        w_ref[a + r] = jnp.broadcast_to(tail[:8, r * B // 2 : r * B // 2 + 1], (8, B))
        if r == 0:
            diagonal = jnp.where(p <= q, mixed, turned)
        else:
            diagonal = jnp.where(p > q, mixed, jnp.where(p < q, turned, tail[8:9]))
        set_x(x_ref, a + r, a + r, diagonal.astype(jnp.bfloat16))
        for k in range(1, 8):
            u = ref[pl.ds(SECOND * r - skip + (k - 1) * B, B)]
            set_x(x_ref, a + r, a + r + k, u)
            if k <= 18 - a - r:
                set_x(x_ref, a + r + k, a + r, u.T)


def square(late, now, x_ref, y_ref, w_ref, part_ref):
    zero = jnp.zeros((B, B), jnp.bfloat16)
    for L in range(4, 10):
        for J in range(L - 4, L + 1):
            terms = square_terms(late, J, L)
            end = max(stage for _, stage in terms)
            if now > end or (now == 0 and end > 0):
                continue
            mine = [m for m, stage in terms if (stage <= now if now < 2 else stage == 2)]
            s = None
            for m, n in runs(mine):
                t = lax.dot_general(
                    x_ref[J, :, blk(m - 2 * J + 7, n)],
                    x_ref[L, :, blk(m - 2 * L + 7, n)],
                    NT,
                    preferred_element_type=jnp.float32,
                )
                s = t if s is None else s + t
            place = L % 3 * 5 + J - L + 4
            if now < end:
                if s is not None:
                    part_ref[place] = s
                continue
            if now == 2 and len(mine) < len(terms):
                s = s + part_ref[place]
            for dj in range(2):
                for dl in range(2):
                    j, l = 2 * J + dj, 2 * L + dl
                    off = abs(l - j)
                    if off > 7 or j in (0, 19) or l in (0, 19):
                        y_ref[blk(j), blk(l - 8)] = zero
                    else:
                        w = w_ref[min(j, l), pl.ds(off, 1)]
                        y_ref[blk(j), blk(l - 8)] = (
                            s[dj * B : (dj + 1) * B, dl * B : (dl + 1) * B] * w
                        ).astype(jnp.bfloat16)


def purify(late, now, x_ref, y_ref, w_ref, part_ref, out, done):
    for I in (4, 5):
        for L in range(I, I + 5):
            terms = cube_terms(late, I, L)
            end = max(stage for _, stage in terms)
            mine = [j for j, stage in terms if (stage == 2) == (now == 2)]
            c = None
            for up in (True, False):
                for j, n in runs([j for j in mine if (j <= 2 * L) == up]):
                    left = x_ref[I, :, blk(j - 2 * I + 7, n)]
                    right = (
                        y_ref[blk(j, n), blk(2 * L - 8, 2)] if up else y_ref[blk(2 * L, 2), blk(j - 8, n)]
                    )
                    t = lax.dot_general(
                        left, right, NN if up else NT, preferred_element_type=jnp.float32
                    )
                    c = t if c is None else c + t
            place = (I - 4) * 5 + L - I
            if now < end:
                if c is not None:
                    part_ref[place] = c
                continue
            if now == 2 and end == 2 and len(mine) < len(terms):
                c = c + part_ref[place]
            for di in range(2):
                for dl in range(2):
                    i, l = 2 * I + di, 2 * L + dl
                    off = l - i
                    if not 0 <= off <= 7:
                        continue
                    if now == 2 and end < 2:
                        out[i - 8, off] = done[i - 8, off]
                        continue
                    w = w_ref[i, pl.ds(off, 1)]
                    sq = y_ref[blk(i), blk(l - 8)].astype(jnp.float32)
                    cube = w * c[di * B : (di + 1) * B, dl * B : (dl + 1) * B]
                    out[i - 8, off] = (3.0 * sq - 2.0 * cube).astype(jnp.bfloat16)


def take_all(x_ref, w_ref, pieces):
    for here, ref, a, rows, skip in pieces:
        pl.when(here)(functools.partial(put, x_ref, w_ref, ref, a, rows, skip))


def for_half(z, z_count, work):
    low = z < z_count // 2
    pl.when(low)(functools.partial(work, LOW))
    pl.when(jnp.logical_not(low))(functools.partial(work, HIGH))


def stage_0(z_count, place, owna, ownb, fw1a, fw1b, bw1a, bw1b, fw2a, fw2b, bw2a, bw2b, x_ref, y_ref, w_ref):
    zero = jnp.zeros((B, B), jnp.bfloat16)
    for c in range(16):
        set_x(x_ref, 0, c - 7, zero)
        set_x(x_ref, 19, c + 11, zero)
    for a in range(1, 19):
        set_x(x_ref, a, a + 8 if a % 2 == 0 else a - 8, zero)
    z = place[0]
    last = z_count - 1
    put(x_ref, w_ref, owna, 8)
    put(x_ref, w_ref, ownb, 10)
    both = (0, 1)
    take_all(
        x_ref,
        w_ref,
        (
            (z > 0, fw1a, 4, both, 0),
            (z > 0, fw1b, 6, both, 0),
            (z < last, bw1a, 12, both, 0),
            (z < last, bw1b, 14, both, 0),
            (z > 1, fw2a, 0, (1,), 0),
            (z > 1, fw2b, 2, both, 0),
            (z < last - 1, bw2a, 16, both, 0),
            (z < last - 1, bw2b, 18, (0,), 0),
        ),
    )

    def work(late):
        square(late, 0, x_ref, y_ref, w_ref, None)

    for_half(z, z_count, work)


def stage_1(z_count, place, x_in, y_in, w_in, ends, cross, x_ref, y_ref, w_ref, sums, cubes, done):
    z = place[0]
    last = z_count - 1
    both = (0, 1)
    take_all(
        x_ref,
        w_ref,
        (
            (z == 0, ends, 6, both, 0),
            (z == last, ends, 12, both, 0),
            (z <= 1, cross, 2, both, 0),
            (z >= last - 1, cross, 16, both, 0),
        ),
    )

    def work(late):
        square(late, 1, x_ref, y_ref, w_ref, sums)
        purify(late, 1, x_ref, y_ref, w_ref, cubes, done, None)

    for_half(z, z_count, work)


def stage_2(z_count, place, x_in, y_in, w_in, sums, cubes, done, ends, cross, out, x_ref, y_ref, w_ref):
    z = place[0]
    last = z_count - 1
    both = (0, 1)
    take_all(
        x_ref,
        w_ref,
        (
            (z == 0, ends, 4, both, 0),
            (z == last, ends, 14, both, 0),
            (z <= 1, cross, 0, (1,), MIXED),
            (z >= last - 1, cross, 18, (0,), 0),
        ),
    )

    def work(late):
        square(late, 2, x_ref, y_ref, w_ref, sums)
        purify(late, 2, x_ref, y_ref, w_ref, cubes, out, done)

    for_half(z, z_count, work)


SMEM = pl.BlockSpec(memory_space=pltpu.SMEM)
VMEM = pl.BlockSpec(memory_space=pltpu.VMEM)
KEPT = [
    pltpu.VMEM((10, 2 * B, 16 * B), jnp.bfloat16),
    pltpu.VMEM((20 * B, 12 * B), jnp.bfloat16),
    pltpu.VMEM((20, 8, B), jnp.float32),
]
PARTIAL = [
    pltpu.VMEM((15, 2 * B, 2 * B), jnp.float32),
    pltpu.VMEM((10, 2 * B, 2 * B), jnp.float32),
    pltpu.VMEM((4, 8, B, B), jnp.bfloat16),
]


def call(kernel, z_count, outs, aliases, flops, *operands):
    return pl.pallas_call(
        functools.partial(kernel, z_count),
        out_shape=outs,
        in_specs=[SMEM] + [VMEM] * (len(operands) - 1),
        out_specs=[VMEM] * len(outs),
        input_output_aliases=aliases,
        compiler_params=pltpu.CompilerParams(vmem_limit_bytes=16 * 1024 * 1024),
        cost_estimate=pl.CostEstimate(flops=flops, bytes_accessed=10**6, transcendentals=0),
    )(*operands)


def compute(z_count, place, rows_0, rows_1, rows_2):
    kept = call(stage_0, z_count, KEPT, {}, 10**9, place, *rows_0)
    got = call(stage_1, z_count, KEPT + PARTIAL, {1: 0, 2: 1, 3: 2}, 6 * 10**9, place, *kept, *rows_1)
    out = [jax.ShapeDtypeStruct((4, 8, B, B), jnp.bfloat16)]
    return call(stage_2, z_count, out + KEPT, {1: 1, 2: 2, 3: 3}, 6 * 10**9, place, *got, *rows_2)[0]


def packed(present, upper, before):
    rows = upper.shape[2]
    pair = jax.ShapeDtypeStruct((PAIR, rows), jnp.bfloat16)
    return pl.pallas_call(
        pack,
        out_shape=[pair, pair],
        in_specs=[SMEM, VMEM, pl.BlockSpec(memory_space=pl.ANY)],
        out_specs=[VMEM, VMEM],
        compiler_params=pltpu.CompilerParams(vmem_limit_bytes=8 * 1024 * 1024),
    )(present, upper, before)


def per_device(upper, present):
    s_count, z_count = lax.axis_size("row"), lax.axis_size("col")
    z = lax.axis_index("col")

    def step(block, d, pairs=None):
        pairs = pairs or [(i, i + d) for i in range(z_count) if 0 <= i + d < z_count]
        return lax.ppermute(block, "col", pairs)

    def hop(block, route):
        pairs = [
            (i * z_count + a, (i + d) % s_count * z_count + b)
            for i in range(s_count)
            for a, d, b in route
        ]
        return lax.ppermute(block, ("row", "col"), pairs)

    last = z_count - 1
    inner = range(1, last)
    parts = packed(present, upper, present)
    again = packed(present, upper, parts[0])
    fw1 = [step(parts[0], 1), step(again[1], 1)]
    bw1 = [step(again[0], -1), step(parts[1], -1)]
    fw2 = [step(part, 1, [(i, i + 1) for i in inner]) for part in fw1]
    bw2 = [step(part, -1, [(i, i - 1) for i in inner]) for part in bw1]
    if z_count == 4:
        to_end, beside = [(1, 1, 0), (2, -1, 3)], [(0, 1, 0), (1, 1, 1), (2, -1, 2), (3, -1, 3)]
        sooner = jnp.where(z < 2, bw2[1], fw2[0])
        ends_first = hop(sooner, to_end)
        cross_first = hop(sooner, beside)
        down, up = lax.optimization_barrier((bw2[0], fw2[1]))
        ends_last = hop(jnp.where(z < 2, down, up), to_end)
        cross_last = hop(jnp.where(z < 2, down[PAIR - ONE :], up[:ONE]), beside)
    else:
        route = [(last, 1, 0), (0, -1, last)]
        ends_first = hop(jnp.where(z == last, parts[1], parts[0]), route)
        ends_last = hop(jnp.where(z == last, parts[0], parts[1]), route)
        route = [(last - 1, 1, 0), (last, 1, 1), (0, -1, last - 1), (1, -1, last)]
        cross_first = hop(jnp.where(z < 2, parts[0], parts[1]), route)
        cross_last = hop(jnp.where(z < 2, parts[1][:ONE], parts[0][PAIR - ONE :]), route)
    rows = (*parts, *fw1, *bw1, *fw2, *bw2)
    return compute(z_count, z.reshape(1), rows, (ends_first, cross_first), (ends_last, cross_last))


def solution(mesh):
    return jax.shard_map(
        per_device,
        mesh=mesh,
        in_specs=(P(("groups", "row", "col"), None, None, None), P(("groups", "row", "col"), None)),
        out_specs=P(("groups", "row", "col"), None, None, None),
        check_vma=False,
    )
```

```python
import functools

import jax
import jax.numpy as jnp
from jax import lax
from jax.experimental import pallas as pl
from jax.experimental.pallas import tpu as pltpu
from jax.sharding import PartitionSpec as P

B = 128
NT = (((1,), (1,)), ((), ()))
NN = (((1,), (0,)), ((), ()))

MIXED = 7 * B
TAIL = 8 * B
SECOND = 8 * B + 16
PAIR = 15 * B + 16
ONE = SECOND

LOW = {1: 2, 2: 1, 3: 1, 4: 2, 5: 2, 6: 1, 7: 1}
HIGH = {12: 1, 13: 1, 14: 2, 15: 2, 16: 1, 17: 1, 18: 2}


def blk(a, n=1):
    return pl.ds(a * B, n * B)


def x_stage(late, J, m):
    return max(late.get(min(2 * J, m), 0), late.get(min(2 * J + 1, m), 0))


def square_terms(late, J, L):
    return [
        (m, max(x_stage(late, J, m), x_stage(late, L, m))) for m in range(2 * L - 7, 2 * J + 9)
    ]


def y_stage(late, J, L):
    return max(stage for _, stage in square_terms(late, min(J, L), max(J, L)))


def cube_terms(late, I, L):
    return [
        (j, max(x_stage(late, I, j), y_stage(late, j // 2, L))) for j in range(2 * L - 7, 2 * I + 9)
    ]


def runs(columns):
    found = []
    for m in columns:
        if found and found[-1][0] + found[-1][1] == m:
            found[-1][1] += 1
        else:
            found.append([m, 1])
    return found


def triangles():
    p = lax.broadcasted_iota(jnp.int32, (B, B), 0)
    q = lax.broadcasted_iota(jnp.int32, (B, B), 1)
    return p, q


def pack(place, present, upper, *outs):
    p, q = triangles()
    right = lax.broadcasted_iota(jnp.int32, (1, B), 1) >= B // 2

    def block(r, k):
        w = present[r, k].astype(jnp.float32)
        return upper[r, k].astype(jnp.float32) * w

    odd = lax.rem(place[0], 2)
    for first, out in zip((2 * odd, 2 - 2 * odd), outs):
        one, two = block(first, 0), block(first + 1, 0)
        out[pl.ds(MIXED, B)] = jnp.where(p <= q, one, two).astype(jnp.bfloat16)
        for r in range(2):
            for k in range(1, 8):
                out[pl.ds(SECOND * r + (k - 1) * B, B)] = block(first + r, k).astype(jnp.bfloat16)
        lines = [
            jnp.where(
                right,
                present[first + 1, k].astype(jnp.float32),
                present[first, k].astype(jnp.float32),
            )
            for k in range(8)
        ]
        lines.append(jnp.sum(jnp.where(p == q, two, 0.0), axis=0, keepdims=True))
        lines.append(jnp.zeros((7, B), jnp.float32))
        out[pl.ds(TAIL, 16)] = jnp.concatenate(lines, axis=0).astype(jnp.bfloat16)


def set_x(x_ref, a, b, value):
    x_ref[a // 2, blk(a % 2), blk(b - a // 2 * 2 + 7)] = value


def put(x_ref, w_ref, ref, a, rows=(0, 1), skip=0):
    p, q = triangles()
    mixed = ref[pl.ds(MIXED - skip, B)].astype(jnp.float32)
    turned = mixed.T
    tail = ref[pl.ds(TAIL - skip, 16)].astype(jnp.float32)
    for r in rows:
        w_ref[a + r] = jnp.broadcast_to(tail[:8, r * B // 2 : r * B // 2 + 1], (8, B))
        if r == 0:
            diagonal = jnp.where(p <= q, mixed, turned)
        else:
            diagonal = jnp.where(p > q, mixed, jnp.where(p < q, turned, tail[8:9]))
        set_x(x_ref, a + r, a + r, diagonal.astype(jnp.bfloat16))
        for k in range(1, 8):
            u = ref[pl.ds(SECOND * r - skip + (k - 1) * B, B)]
            set_x(x_ref, a + r, a + r + k, u)
            if k <= 18 - a - r:
                set_x(x_ref, a + r + k, a + r, u.T)


def square(late, now, x_ref, y_ref, w_ref, part_ref):
    zero = jnp.zeros((B, B), jnp.bfloat16)
    for L in range(4, 10):
        for J in range(L - 4, L + 1):
            terms = square_terms(late, J, L)
            end = max(stage for _, stage in terms)
            if now > end or (now == 0 and end > 0):
                continue
            mine = [m for m, stage in terms if (stage <= now if now < 2 else stage == 2)]
            s = None
            for m, n in runs(mine):
                t = lax.dot_general(
                    x_ref[J, :, blk(m - 2 * J + 7, n)],
                    x_ref[L, :, blk(m - 2 * L + 7, n)],
                    NT,
                    preferred_element_type=jnp.float32,
                )
                s = t if s is None else s + t
            place = L % 3 * 5 + J - L + 4
            if now < end:
                if s is not None:
                    part_ref[place] = s
                continue
            if now == 2 and len(mine) < len(terms):
                s = s + part_ref[place]
            for dj in range(2):
                for dl in range(2):
                    j, l = 2 * J + dj, 2 * L + dl
                    off = abs(l - j)
                    if off > 7 or j in (0, 19) or l in (0, 19):
                        y_ref[blk(j), blk(l - 8)] = zero
                    else:
                        w = w_ref[min(j, l), pl.ds(off, 1)]
                        y_ref[blk(j), blk(l - 8)] = (
                            s[dj * B : (dj + 1) * B, dl * B : (dl + 1) * B] * w
                        ).astype(jnp.bfloat16)


def purify(late, now, x_ref, y_ref, w_ref, part_ref, out, done):
    for I in (4, 5):
        for L in range(I, I + 5):
            terms = cube_terms(late, I, L)
            end = max(stage for _, stage in terms)
            mine = [j for j, stage in terms if (stage == 2) == (now == 2)]
            c = None
            for up in (True, False):
                for j, n in runs([j for j in mine if (j <= 2 * L) == up]):
                    left = x_ref[I, :, blk(j - 2 * I + 7, n)]
                    right = (
                        y_ref[blk(j, n), blk(2 * L - 8, 2)] if up else y_ref[blk(2 * L, 2), blk(j - 8, n)]
                    )
                    t = lax.dot_general(
                        left, right, NN if up else NT, preferred_element_type=jnp.float32
                    )
                    c = t if c is None else c + t
            place = (I - 4) * 5 + L - I
            if now < end:
                if c is not None:
                    part_ref[place] = c
                continue
            if now == 2 and end == 2 and len(mine) < len(terms):
                c = c + part_ref[place]
            for di in range(2):
                for dl in range(2):
                    i, l = 2 * I + di, 2 * L + dl
                    off = l - i
                    if not 0 <= off <= 7:
                        continue
                    if now == 2 and end < 2:
                        out[i - 8, off] = done[i - 8, off]
                        continue
                    w = w_ref[i, pl.ds(off, 1)]
                    sq = y_ref[blk(i), blk(l - 8)].astype(jnp.float32)
                    cube = w * c[di * B : (di + 1) * B, dl * B : (dl + 1) * B]
                    out[i - 8, off] = (3.0 * sq - 2.0 * cube).astype(jnp.bfloat16)


def take_all(x_ref, w_ref, pieces):
    for here, ref, a, rows, skip in pieces:
        pl.when(here)(functools.partial(put, x_ref, w_ref, ref, a, rows, skip))


def for_half(z, z_count, work):
    low = z < z_count // 2
    pl.when(low)(functools.partial(work, LOW))
    pl.when(jnp.logical_not(low))(functools.partial(work, HIGH))


def stage_0(z_count, place, own1, own2, a1, a2, b1, b2, ra1, ra2, rb1, rb2, x_ref, y_ref, w_ref):
    zero = jnp.zeros((B, B), jnp.bfloat16)
    for c in range(16):
        set_x(x_ref, 0, c - 7, zero)
        set_x(x_ref, 19, c + 11, zero)
    for a in range(1, 19):
        set_x(x_ref, a, a + 8 if a % 2 == 0 else a - 8, zero)
    z = place[0]
    last = z_count - 1
    both = (0, 1)
    even = lax.rem(z, 2) == 0
    for here, (owna, ownb, fw1a, fw1b, bw1a, bw1b, fw2a, fw2b, bw2a, bw2b) in (
        (even, (own1, own2, b1, b2, a2, a1, rb1, rb2, ra2, ra1)),
        (jnp.logical_not(even), (own2, own1, a1, a2, b2, b1, ra1, ra2, rb2, rb1)),
    ):
        take_all(
            x_ref,
            w_ref,
            (
                (here, owna, 8, both, 0),
                (here, ownb, 10, both, 0),
                (here & (z > 0), fw1a, 4, both, 0),
                (here & (z > 0), fw1b, 6, both, 0),
                (here & (z < last), bw1a, 12, both, 0),
                (here & (z < last), bw1b, 14, both, 0),
                (here & (z > 1), fw2a, 0, (1,), 0),
                (here & (z > 1), fw2b, 2, both, 0),
                (here & (z < last - 1), bw2a, 16, both, 0),
                (here & (z < last - 1), bw2b, 18, (0,), 0),
            ),
        )

    def work(late):
        square(late, 0, x_ref, y_ref, w_ref, None)

    for_half(z, z_count, work)


def stage_1(z_count, place, x_in, y_in, w_in, ends, cross, x_ref, y_ref, w_ref, sums, cubes, done):
    z = place[0]
    last = z_count - 1
    both = (0, 1)
    take_all(
        x_ref,
        w_ref,
        (
            (z == 0, ends, 6, both, 0),
            (z == last, ends, 12, both, 0),
            (z <= 1, cross, 2, both, 0),
            (z >= last - 1, cross, 16, both, 0),
        ),
    )

    def work(late):
        square(late, 1, x_ref, y_ref, w_ref, sums)
        purify(late, 1, x_ref, y_ref, w_ref, cubes, done, None)

    for_half(z, z_count, work)


def stage_2(z_count, place, x_in, y_in, w_in, sums, cubes, done, ends, cross, out, x_ref, y_ref, w_ref):
    z = place[0]
    last = z_count - 1
    both = (0, 1)
    take_all(
        x_ref,
        w_ref,
        (
            (z == 0, ends, 4, both, 0),
            (z == last, ends, 14, both, 0),
            (z <= 1, cross, 0, (1,), MIXED),
            (z >= last - 1, cross, 18, (0,), 0),
        ),
    )

    def work(late):
        square(late, 2, x_ref, y_ref, w_ref, sums)
        purify(late, 2, x_ref, y_ref, w_ref, cubes, out, done)

    for_half(z, z_count, work)


SMEM = pl.BlockSpec(memory_space=pltpu.SMEM)
VMEM = pl.BlockSpec(memory_space=pltpu.VMEM)
KEPT = [
    pltpu.VMEM((10, 2 * B, 16 * B), jnp.bfloat16),
    pltpu.VMEM((20 * B, 12 * B), jnp.bfloat16),
    pltpu.VMEM((20, 8, B), jnp.float32),
]
PARTIAL = [
    pltpu.VMEM((15, 2 * B, 2 * B), jnp.float32),
    pltpu.VMEM((10, 2 * B, 2 * B), jnp.float32),
    pltpu.VMEM((4, 8, B, B), jnp.bfloat16),
]


def call(kernel, z_count, outs, aliases, flops, *operands):
    return pl.pallas_call(
        functools.partial(kernel, z_count),
        out_shape=outs,
        in_specs=[SMEM] + [VMEM] * (len(operands) - 1),
        out_specs=[VMEM] * len(outs),
        input_output_aliases=aliases,
        compiler_params=pltpu.CompilerParams(vmem_limit_bytes=16 * 1024 * 1024),
        cost_estimate=pl.CostEstimate(flops=flops, bytes_accessed=10**6, transcendentals=0),
    )(*operands)


def compute(z_count, place, rows_0, rows_1, rows_2):
    kept = call(stage_0, z_count, KEPT, {}, 10**9, place, *rows_0)
    got = call(stage_1, z_count, KEPT + PARTIAL, {1: 0, 2: 1, 3: 2}, 6 * 10**9, place, *kept, *rows_1)
    out = [jax.ShapeDtypeStruct((4, 8, B, B), jnp.bfloat16)]
    return call(stage_2, z_count, out + KEPT, {1: 1, 2: 2, 3: 3}, 6 * 10**9, place, *got, *rows_2)[0]


def copy_pairs(one, two, out_one, out_two):
    out_one[...] = one[...]
    out_two[...] = two[...]


def pair_call(kernel, limit, specs, *operands):
    pair = jax.ShapeDtypeStruct((PAIR, B), jnp.bfloat16)
    return pl.pallas_call(
        kernel,
        out_shape=[pair, pair],
        in_specs=specs,
        out_specs=[VMEM, VMEM],
        compiler_params=pltpu.CompilerParams(vmem_limit_bytes=limit * 1024 * 1024),
    )(*operands)


def per_device(upper, present):
    s_count, z_count = lax.axis_size("row"), lax.axis_size("col")
    z = lax.axis_index("col")
    place = z.reshape(1)
    last = z_count - 1

    def swap(block, odd, inner=False):
        pairs = [(i, i + 1) for i in range(odd, last, 2)]
        pairs += [(j, i) for i, j in pairs]
        pairs = [pair for pair in pairs if not (inner and pair[0] in (0, last))]
        return lax.ppermute(block, "col", pairs)

    def hop(block, route):
        pairs = [
            (i * z_count + a, (i + d) % s_count * z_count + b)
            for i in range(s_count)
            for a, d, b in route
        ]
        return lax.ppermute(block, ("row", "col"), pairs)

    own = pair_call(pack, 40, [SMEM, SMEM, VMEM], place, present, upper)
    again = pair_call(copy_pairs, 8, [VMEM, VMEM], *own)
    a1, b1 = swap(own[0], 0), swap(own[1], 1)
    a2, b2 = swap(again[1], 0), swap(again[0], 1)
    ra1, rb1 = swap(b1, 0, True), swap(a1, 1)
    ra2, rb2 = swap(b2, 0, True), swap(a2, 1)
    edge = (z == 0) | (z == last)
    if z_count == 4:
        to_end, beside = [(1, 1, 0), (2, -1, 3)], [(0, 1, 0), (1, 1, 1), (2, -1, 2), (3, -1, 3)]
        ends_first = hop(rb1, to_end)
        cross_first = hop(jnp.where(edge, ra1, rb1), beside)
        ends_last = hop(rb2, to_end)
        later = jnp.where(edge, ra2, rb2)
        cross_last = hop(jnp.where(z < 2, later[PAIR - ONE :], later[:ONE]), beside)
    else:
        route = [(last, 1, 0), (0, -1, last)]
        ends_first, ends_last = hop(own[0], route), hop(own[1], route)
        route = [(last - 1, 1, 0), (last, 1, 1), (0, -1, last - 1), (1, -1, last)]
        cross_first = hop(jnp.where(edge, own[0], own[1]), route)
        later = jnp.where(edge, own[1], own[0])
        cross_last = hop(jnp.where(z < 2, later[:ONE], later[PAIR - ONE :]), route)
    rows = (*own, a1, a2, b1, b2, ra1, ra2, rb1, rb2)
    return compute(z_count, place, rows, (ends_first, cross_first), (ends_last, cross_last))


def solution(mesh):
    return jax.shard_map(
        per_device,
        mesh=mesh,
        in_specs=(P(("groups", "row", "col"), None, None, None), P(("groups", "row", "col"), None)),
        out_specs=P(("groups", "row", "col"), None, None, None),
        check_vma=False,
    )
```

```python
import functools

import jax
import jax.numpy as jnp
from jax import lax
from jax.experimental import pallas as pl
from jax.experimental.pallas import tpu as pltpu
from jax.sharding import PartitionSpec as P

B = 128
NT = (((1,), (1,)), ((), ()))
NN = (((1,), (0,)), ((), ()))

MIXED = 7 * B
TAIL = 8 * B
SECOND = 8 * B + 16
PAIR = 15 * B + 16
ONE = SECOND

LOW = {1: 1, 2: 1, 3: 1, 4: 2, 5: 2, 6: 1, 7: 1}
HIGH = {12: 1, 13: 1, 14: 2, 15: 2, 16: 1, 17: 1, 18: 1}


def blk(a, n=1):
    return pl.ds(a * B, n * B)


def x_stage(late, J, m):
    return max(late.get(min(2 * J, m), 0), late.get(min(2 * J + 1, m), 0))


def square_terms(late, J, L):
    return [
        (m, max(x_stage(late, J, m), x_stage(late, L, m))) for m in range(2 * L - 7, 2 * J + 9)
    ]


def y_stage(late, J, L):
    return max(stage for _, stage in square_terms(late, min(J, L), max(J, L)))


def cube_terms(late, I, L):
    return [
        (j, max(x_stage(late, I, j), y_stage(late, j // 2, L))) for j in range(2 * L - 7, 2 * I + 9)
    ]


def runs(columns):
    found = []
    for m in columns:
        if found and found[-1][0] + found[-1][1] == m:
            found[-1][1] += 1
        else:
            found.append([m, 1])
    return found


def triangles():
    p = lax.broadcasted_iota(jnp.int32, (B, B), 0)
    q = lax.broadcasted_iota(jnp.int32, (B, B), 1)
    return p, q


def pack(present, upper, *outs):
    p, q = triangles()
    right = lax.broadcasted_iota(jnp.int32, (1, B), 1) >= B // 2

    def block(r, k):
        w = present[r, k].astype(jnp.float32)
        return upper[r, k].astype(jnp.float32) * w

    odd = lax.rem(lax.axis_index("col"), 2)
    for first, out in zip((2 * odd, 2 - 2 * odd), outs):
        one, two = block(first, 0), block(first + 1, 0)
        out[pl.ds(MIXED, B)] = jnp.where(p <= q, one, two).astype(jnp.bfloat16)
        for r in range(2):
            for k in range(1, 8):
                out[pl.ds(SECOND * r + (k - 1) * B, B)] = block(first + r, k).astype(jnp.bfloat16)
        lines = [
            jnp.where(
                right,
                present[first + 1, k].astype(jnp.float32),
                present[first, k].astype(jnp.float32),
            )
            for k in range(8)
        ]
        lines.append(jnp.sum(jnp.where(p == q, two, 0.0), axis=0, keepdims=True))
        lines.append(jnp.zeros((7, B), jnp.float32))
        out[pl.ds(TAIL, 16)] = jnp.concatenate(lines, axis=0).astype(jnp.bfloat16)


def set_x(x_ref, a, b, value):
    x_ref[a // 2, blk(a % 2), blk(b - a // 2 * 2 + 7)] = value


def put(x_ref, w_ref, ref, a, rows=(0, 1), skip=0):
    p, q = triangles()
    mixed = ref[pl.ds(MIXED - skip, B)].astype(jnp.float32)
    turned = mixed.T
    tail = ref[pl.ds(TAIL - skip, 16)].astype(jnp.float32)
    for r in rows:
        w_ref[a + r] = jnp.broadcast_to(tail[:8, r * B // 2 : r * B // 2 + 1], (8, B))
        if r == 0:
            diagonal = jnp.where(p <= q, mixed, turned)
        else:
            diagonal = jnp.where(p > q, mixed, jnp.where(p < q, turned, tail[8:9]))
        set_x(x_ref, a + r, a + r, diagonal.astype(jnp.bfloat16))
        for k in range(1, 8):
            u = ref[pl.ds(SECOND * r - skip + (k - 1) * B, B)]
            set_x(x_ref, a + r, a + r + k, u)
            if k <= 18 - a - r:
                set_x(x_ref, a + r + k, a + r, u.T)


def square(late, now, x_ref, y_ref, w_ref, part_ref):
    zero = jnp.zeros((B, B), jnp.bfloat16)
    for L in range(4, 10):
        for J in range(L - 4, L + 1):
            terms = square_terms(late, J, L)
            end = max(stage for _, stage in terms)
            if now > end or (now == 0 and end > 0):
                continue
            mine = [m for m, stage in terms if (stage <= now if now < 2 else stage == 2)]
            s = None
            for m, n in runs(mine):
                t = lax.dot_general(
                    x_ref[J, :, blk(m - 2 * J + 7, n)],
                    x_ref[L, :, blk(m - 2 * L + 7, n)],
                    NT,
                    preferred_element_type=jnp.float32,
                )
                s = t if s is None else s + t
            place = L % 3 * 5 + J - L + 4
            if now < end:
                if s is not None:
                    part_ref[place] = s
                continue
            if now == 2 and len(mine) < len(terms):
                s = s + part_ref[place]
            for dj in range(2):
                for dl in range(2):
                    j, l = 2 * J + dj, 2 * L + dl
                    off = abs(l - j)
                    if off > 7 or j in (0, 19) or l in (0, 19):
                        y_ref[blk(j), blk(l - 8)] = zero
                    else:
                        w = w_ref[min(j, l), pl.ds(off, 1)]
                        y_ref[blk(j), blk(l - 8)] = (
                            s[dj * B : (dj + 1) * B, dl * B : (dl + 1) * B] * w
                        ).astype(jnp.bfloat16)


def purify(late, now, x_ref, y_ref, w_ref, part_ref, ready, send=None):
    for I in (4, 5):
        for L in range(I, I + 5):
            terms = cube_terms(late, I, L)
            end = max(stage for _, stage in terms)
            mine = [j for j, stage in terms if (stage == 2) == (now == 2)]
            c = None
            for up in (True, False):
                for j, n in runs([j for j in mine if (j <= 2 * L) == up]):
                    left = x_ref[I, :, blk(j - 2 * I + 7, n)]
                    right = (
                        y_ref[blk(j, n), blk(2 * L - 8, 2)] if up else y_ref[blk(2 * L, 2), blk(j - 8, n)]
                    )
                    t = lax.dot_general(
                        left, right, NN if up else NT, preferred_element_type=jnp.float32
                    )
                    c = t if c is None else c + t
            place = (I - 4) * 5 + L - I
            if now < end:
                if c is not None:
                    part_ref[place] = c
                continue
            if now == 2 and end == 2 and len(mine) < len(terms):
                c = c + part_ref[place]
            for di in range(2):
                i = 2 * I + di
                offsets = [off for off in (2 * L - i, 2 * L + 1 - i) if 0 <= off <= 7]
                if not offsets:
                    continue
                for off in offsets:
                    if now == 2 and end < 2:
                        break
                    l = i + off
                    dl = l - 2 * L
                    w = w_ref[i, pl.ds(off, 1)]
                    sq = y_ref[blk(i), blk(l - 8)].astype(jnp.float32)
                    cube = w * c[di * B : (di + 1) * B, dl * B : (dl + 1) * B]
                    ready[i - 8, off] = (3.0 * sq - 2.0 * cube).astype(jnp.bfloat16)
                if send is not None:
                    send(end < 2, (place, di), i - 8, offsets[0], len(offsets))


def take_all(x_ref, w_ref, pieces):
    for here, ref, a, rows, skip in pieces:
        pl.when(here)(functools.partial(put, x_ref, w_ref, ref, a, rows, skip))


def for_half(z, z_count, work):
    low = z < z_count // 2
    pl.when(low)(functools.partial(work, LOW))
    pl.when(jnp.logical_not(low))(functools.partial(work, HIGH))


def stage_0(z_count, own1, own2, a1, a2, b1, b2, ra1, ra2, rb1, rb2, x_ref, y_ref, w_ref):
    zero = jnp.zeros((B, B), jnp.bfloat16)
    for c in range(16):
        set_x(x_ref, 0, c - 7, zero)
        set_x(x_ref, 19, c + 11, zero)
    for a in range(1, 19):
        set_x(x_ref, a, a + 8 if a % 2 == 0 else a - 8, zero)
    z = lax.axis_index("col")
    last = z_count - 1
    both = (0, 1)
    even = lax.rem(z, 2) == 0
    for here, (owna, ownb, fw1a, fw1b, bw1a, bw1b, fw2a, fw2b, bw2a, bw2b) in (
        (even, (own1, own2, b1, b2, a2, a1, rb1, rb2, ra2, ra1)),
        (jnp.logical_not(even), (own2, own1, a1, a2, b2, b1, ra1, ra2, rb2, rb1)),
    ):
        take_all(
            x_ref,
            w_ref,
            (
                (here, owna, 8, both, 0),
                (here, ownb, 10, both, 0),
                (here & (z > 0), fw1a, 4, both, 0),
                (here & (z > 0), fw1b, 6, both, 0),
                (here & (z < last), bw1a, 12, both, 0),
                (here & (z < last), bw1b, 14, both, 0),
                (here & (z > 1), fw2a, 0, (1,), 0),
                (here & (z > 1), fw2b, 2, both, 0),
                (here & (z < last - 1), bw2a, 16, both, 0),
                (here & (z < last - 1), bw2b, 18, (0,), 0),
            ),
        )

    def work(late):
        square(late, 0, x_ref, y_ref, w_ref, None)

    for_half(z, z_count, work)


def stage_1(z_count, x_in, y_in, w_in, ends, cross, line, x_ref, y_ref, w_ref, sums, cubes, done):
    z = lax.axis_index("col")
    last = z_count - 1
    both = (0, 1)
    take_all(
        x_ref,
        w_ref,
        (
            (z == 0, ends, 6, both, 0),
            (z == last, ends, 12, both, 0),
            (z <= 1, cross, 2, both, 0),
            (z >= last - 1, cross, 16, both, 0),
            (z <= 1, line, 0, (1,), MIXED),
            (z >= last - 1, line, 18, (0,), 0),
        ),
    )

    def work(late):
        square(late, 1, x_ref, y_ref, w_ref, sums)
        purify(late, 1, x_ref, y_ref, w_ref, cubes, done)

    for_half(z, z_count, work)


def stage_2(z_count, x_in, y_in, w_in, sums, cubes, done, ends, x_ref, y_ref, w_ref, out, ready, sems):
    z = lax.axis_index("col")
    last = z_count - 1
    both = (0, 1)
    take_all(
        x_ref,
        w_ref,
        (
            (z == 0, ends, 4, both, 0),
            (z == last, ends, 14, both, 0),
        ),
    )

    def work(late):
        copies = []

        def send(early, place, i, offset, count):
            part = pl.ds(offset, count)
            copy = pltpu.make_async_copy(
                (done if early else ready).at[i, part], out.at[i, part], sems.at[place]
            )
            copy.start()
            copies.append(copy)

        square(late, 2, x_ref, y_ref, w_ref, sums)
        purify(late, 2, x_ref, y_ref, w_ref, cubes, ready, send)
        for copy in copies:
            copy.wait()

    for_half(z, z_count, work)


SMEM = pl.BlockSpec(memory_space=pltpu.SMEM)
VMEM = pl.BlockSpec(memory_space=pltpu.VMEM)
KEPT = [
    pltpu.VMEM((10, 2 * B, 16 * B), jnp.bfloat16),
    pltpu.VMEM((20 * B, 12 * B), jnp.bfloat16),
    pltpu.VMEM((20, 8, B), jnp.float32),
]
PARTIAL = [
    pltpu.VMEM((15, 2 * B, 2 * B), jnp.float32),
    pltpu.VMEM((10, 2 * B, 2 * B), jnp.float32),
    pltpu.VMEM((4, 8, B, B), jnp.bfloat16),
]


def call(kernel, z_count, outs, specs, aliases, scratch, flops, *operands):
    return pl.pallas_call(
        functools.partial(kernel, z_count),
        out_shape=outs,
        in_specs=[VMEM] * len(operands),
        out_specs=specs,
        input_output_aliases=aliases,
        scratch_shapes=scratch,
        compiler_params=pltpu.CompilerParams(vmem_limit_bytes=16 * 1024 * 1024),
        cost_estimate=pl.CostEstimate(flops=flops, bytes_accessed=10**6, transcendentals=0),
    )(*operands)


def compute(z_count, rows_0, rows_1, rows_2):
    kept = call(stage_0, z_count, KEPT, [VMEM] * 3, {}, [], 10**9, *rows_0)
    aliases = {0: 0, 1: 1, 2: 2}
    outs = KEPT + PARTIAL
    got = call(stage_1, z_count, outs, [VMEM] * 6, aliases, [], 6 * 10**9, *kept, *rows_1)
    outs = KEPT + [jax.ShapeDtypeStruct((4, 8, B, B), jnp.bfloat16)]
    specs = [VMEM] * 3 + [pl.BlockSpec(memory_space=pl.ANY)]
    scratch = [pltpu.VMEM((4, 8, B, B), jnp.bfloat16), pltpu.SemaphoreType.DMA((10, 2))]
    return call(stage_2, z_count, outs, specs, aliases, scratch, 6 * 10**9, *got, *rows_2)[3]


def copy_pairs(one, two, out_one, out_two):
    out_one[...] = one[...]
    out_two[...] = two[...]


def pair_call(kernel, limit, specs, *operands):
    pair = jax.ShapeDtypeStruct((PAIR, B), jnp.bfloat16)
    return pl.pallas_call(
        kernel,
        out_shape=[pair, pair],
        in_specs=specs,
        out_specs=[VMEM, VMEM],
        compiler_params=pltpu.CompilerParams(vmem_limit_bytes=limit * 1024 * 1024),
    )(*operands)


def per_device(upper, present):
    s_count, z_count = lax.axis_size("row"), lax.axis_size("col")
    z = lax.axis_index("col")
    last = z_count - 1

    def swap(block, odd, inner=False):
        pairs = [(i, i + 1) for i in range(odd, last, 2)]
        pairs += [(j, i) for i, j in pairs]
        pairs = [pair for pair in pairs if not (inner and pair[0] in (0, last))]
        return lax.ppermute(block, "col", pairs)

    def hop(block, route):
        pairs = [
            (i * z_count + a, (i + d) % s_count * z_count + b)
            for i in range(s_count)
            for a, d, b in route
        ]
        return lax.ppermute(block, ("row", "col"), pairs)

    own = pair_call(pack, 60, [SMEM, VMEM], present, upper)
    again = pair_call(copy_pairs, 8, [VMEM, VMEM], *own)
    a1, b1 = swap(own[0], 0), swap(own[1], 1)
    a2, b2 = swap(again[1], 0), swap(again[0], 1)
    ra1, rb1 = swap(b1, 0, True), swap(a1, 1)
    ra2, rb2 = swap(b2, 0, True), swap(a2, 1)
    edge = (z == 0) | (z == last)
    if z_count == 4:
        to_end, beside = [(1, 1, 0), (2, -1, 3)], [(0, 1, 0), (1, 1, 1), (2, -1, 2), (3, -1, 3)]
        ends_first = hop(rb1, to_end)
        cross_first = hop(jnp.where(edge, ra1, rb1), beside)
        ends_last = hop(rb2, to_end)
        later = jnp.where(edge, ra2, rb2)
        cross_last = hop(jnp.where(z < 2, later[PAIR - ONE :], later[:ONE]), beside)
    else:
        route = [(last, 1, 0), (0, -1, last)]
        ends_first, ends_last = hop(own[0], route), hop(own[1], route)
        route = [(last - 1, 1, 0), (last, 1, 1), (0, -1, last - 1), (1, -1, last)]
        cross_first = hop(jnp.where(edge, own[0], own[1]), route)
        later = jnp.where(edge, own[1], own[0])
        cross_last = hop(jnp.where(z < 2, later[:ONE], later[PAIR - ONE :]), route)
    rows = (*own, a1, a2, b1, b2, ra1, ra2, rb1, rb2)
    return compute(z_count, rows, (ends_first, cross_first, cross_last), (ends_last,))


def solution(mesh):
    return jax.shard_map(
        per_device,
        mesh=mesh,
        in_specs=(P(("groups", "row", "col"), None, None, None), P(("groups", "row", "col"), None)),
        out_specs=P(("groups", "row", "col"), None, None, None),
        check_vma=False,
    )
```

```python
import functools

import jax
import jax.numpy as jnp
from jax import lax
from jax.experimental import pallas as pl
from jax.experimental.pallas import tpu as pltpu
from jax.sharding import PartitionSpec as P

B = 128
NT = (((1,), (1,)), ((), ()))
NN = (((1,), (0,)), ((), ()))

MIXED = 7 * B
TAIL = 8 * B
SECOND = 8 * B + 16
PAIR = 15 * B + 16
ONE = SECOND

LOW = {1: 1, 2: 1, 3: 1, 4: 2, 5: 2, 6: 1, 7: 1}
HIGH = {12: 1, 13: 1, 14: 2, 15: 2, 16: 1, 17: 1, 18: 1}


def blk(a, n=1):
    return pl.ds(a * B, n * B)


def x_stage(late, J, m):
    return max(late.get(min(2 * J, m), 0), late.get(min(2 * J + 1, m), 0))


def square_terms(late, J, L):
    return [
        (m, max(x_stage(late, J, m), x_stage(late, L, m))) for m in range(2 * L - 7, 2 * J + 9)
    ]


def y_stage(late, J, L):
    return max(stage for _, stage in square_terms(late, min(J, L), max(J, L)))


def cube_terms(late, I, L):
    return [
        (j, max(x_stage(late, I, j), y_stage(late, j // 2, L))) for j in range(2 * L - 7, 2 * I + 9)
    ]


def runs(columns):
    found = []
    for m in columns:
        if found and found[-1][0] + found[-1][1] == m:
            found[-1][1] += 1
        else:
            found.append([m, 1])
    return found


def triangles():
    p = lax.broadcasted_iota(jnp.int32, (B, B), 0)
    q = lax.broadcasted_iota(jnp.int32, (B, B), 1)
    return p, q


def pack(present, upper_hbm, one, two, upper, sems):
    p, q = triangles()
    right = lax.broadcasted_iota(jnp.int32, (1, B), 1) >= B // 2

    def block(r, k):
        w = present[r, k].astype(jnp.float32)
        return upper[r, k].astype(jnp.float32) * w

    odd = lax.rem(lax.axis_index("col"), 2)
    halves = (2 * odd, 2 - 2 * odd)
    copies = []
    for n, first in enumerate(halves):
        part = pl.ds(first, 2)
        copies.append(pltpu.make_async_copy(upper_hbm.at[part], upper.at[part], sems.at[n]))
        copies[-1].start()
    for first, out, copy in zip(halves, (one, two), copies):
        copy.wait()
        one, two = block(first, 0), block(first + 1, 0)
        out[pl.ds(MIXED, B)] = jnp.where(p <= q, one, two).astype(jnp.bfloat16)
        for r in range(2):
            for k in range(1, 8):
                out[pl.ds(SECOND * r + (k - 1) * B, B)] = block(first + r, k).astype(jnp.bfloat16)
        lines = [
            jnp.where(
                right,
                present[first + 1, k].astype(jnp.float32),
                present[first, k].astype(jnp.float32),
            )
            for k in range(8)
        ]
        lines.append(jnp.sum(jnp.where(p == q, two, 0.0), axis=0, keepdims=True))
        lines.append(jnp.zeros((7, B), jnp.float32))
        out[pl.ds(TAIL, 16)] = jnp.concatenate(lines, axis=0).astype(jnp.bfloat16)


def set_x(x_ref, a, b, value):
    x_ref[a // 2, blk(a % 2), blk(b - a // 2 * 2 + 7)] = value


def put(x_ref, w_ref, ref, a, rows=(0, 1), skip=0):
    p, q = triangles()
    mixed = ref[pl.ds(MIXED - skip, B)].astype(jnp.float32)
    turned = mixed.T
    tail = ref[pl.ds(TAIL - skip, 16)].astype(jnp.float32)
    for r in rows:
        w_ref[a + r] = jnp.broadcast_to(tail[:8, r * B // 2 : r * B // 2 + 1], (8, B))
        if r == 0:
            diagonal = jnp.where(p <= q, mixed, turned)
        else:
            diagonal = jnp.where(p > q, mixed, jnp.where(p < q, turned, tail[8:9]))
        set_x(x_ref, a + r, a + r, diagonal.astype(jnp.bfloat16))
        for k in range(1, 8):
            u = ref[pl.ds(SECOND * r - skip + (k - 1) * B, B)]
            set_x(x_ref, a + r, a + r + k, u)
            if k <= 18 - a - r:
                set_x(x_ref, a + r + k, a + r, u.T)


def square(late, now, x_ref, y_ref, w_ref, part_ref):
    zero = jnp.zeros((B, B), jnp.bfloat16)
    for L in range(4, 10):
        for J in range(L - 4, L + 1):
            terms = square_terms(late, J, L)
            end = max(stage for _, stage in terms)
            if now > end or (now == 0 and end > 0):
                continue
            mine = [m for m, stage in terms if (stage <= now if now < 2 else stage == 2)]
            s = None
            for m, n in runs(mine):
                t = lax.dot_general(
                    x_ref[J, :, blk(m - 2 * J + 7, n)],
                    x_ref[L, :, blk(m - 2 * L + 7, n)],
                    NT,
                    preferred_element_type=jnp.float32,
                )
                s = t if s is None else s + t
            place = L % 3 * 5 + J - L + 4
            if now < end:
                if s is not None:
                    part_ref[place] = s
                continue
            if now == 2 and len(mine) < len(terms):
                s = s + part_ref[place]
            for dj in range(2):
                for dl in range(2):
                    j, l = 2 * J + dj, 2 * L + dl
                    off = abs(l - j)
                    if off > 7 or j in (0, 19) or l in (0, 19):
                        y_ref[blk(j), blk(l - 8)] = zero
                    else:
                        w = w_ref[min(j, l), pl.ds(off, 1)]
                        y_ref[blk(j), blk(l - 8)] = (
                            s[dj * B : (dj + 1) * B, dl * B : (dl + 1) * B] * w
                        ).astype(jnp.bfloat16)


def purify(late, now, x_ref, y_ref, w_ref, part_ref, ready, send=None):
    for I in (4, 5):
        complete = {}
        for L in range(I, I + 5):
            terms = cube_terms(late, I, L)
            end = max(stage for _, stage in terms)
            mine = [j for j, stage in terms if (stage == 2) == (now == 2)]
            c = None
            for up in (True, False):
                for j, n in runs([j for j in mine if (j <= 2 * L) == up]):
                    left = x_ref[I, :, blk(j - 2 * I + 7, n)]
                    right = (
                        y_ref[blk(j, n), blk(2 * L - 8, 2)] if up else y_ref[blk(2 * L, 2), blk(j - 8, n)]
                    )
                    t = lax.dot_general(
                        left, right, NN if up else NT, preferred_element_type=jnp.float32
                    )
                    c = t if c is None else c + t
            place = (I - 4) * 5 + L - I
            if now < end:
                if c is not None:
                    part_ref[place] = c
                continue
            if now == 2 and end == 2 and len(mine) < len(terms):
                c = c + part_ref[place]
            for di in range(2):
                i = 2 * I + di
                offsets = [off for off in (2 * L - i, 2 * L + 1 - i) if 0 <= off <= 7]
                if not offsets:
                    continue
                for off in offsets:
                    if now == 2 and end < 2:
                        break
                    l = i + off
                    dl = l - 2 * L
                    w = w_ref[i, pl.ds(off, 1)]
                    sq = y_ref[blk(i), blk(l - 8)].astype(jnp.float32)
                    cube = w * c[di * B : (di + 1) * B, dl * B : (dl + 1) * B]
                    ready[i - 8, off] = (3.0 * sq - 2.0 * cube).astype(jnp.bfloat16)
                complete.setdefault((i - 8, end < 2), []).extend(offsets)
        if send is not None:
            for (i, early), offsets in complete.items():
                send(i, int(early), min(offsets), len(offsets))


def take_all(x_ref, w_ref, pieces):
    for here, ref, a, rows, skip in pieces:
        pl.when(here)(functools.partial(put, x_ref, w_ref, ref, a, rows, skip))


def for_half(z, z_count, work):
    low = z < z_count // 2
    pl.when(low)(functools.partial(work, LOW))
    pl.when(jnp.logical_not(low))(functools.partial(work, HIGH))


def stage_0(z_count, own1, own2, a1, a2, b1, b2, ra1, ra2, rb1, rb2, x_ref, y_ref, w_ref):
    zero = jnp.zeros((B, B), jnp.bfloat16)
    for c in range(16):
        set_x(x_ref, 0, c - 7, zero)
        set_x(x_ref, 19, c + 11, zero)
    for a in range(1, 19):
        set_x(x_ref, a, a + 8 if a % 2 == 0 else a - 8, zero)
    z = lax.axis_index("col")
    last = z_count - 1
    both = (0, 1)
    even = lax.rem(z, 2) == 0
    for here, (owna, ownb, fw1a, fw1b, bw1a, bw1b, fw2a, fw2b, bw2a, bw2b) in (
        (even, (own1, own2, b1, b2, a2, a1, rb1, rb2, ra2, ra1)),
        (jnp.logical_not(even), (own2, own1, a1, a2, b2, b1, ra1, ra2, rb2, rb1)),
    ):
        take_all(
            x_ref,
            w_ref,
            (
                (here, owna, 8, both, 0),
                (here, ownb, 10, both, 0),
                (here & (z > 0), fw1a, 4, both, 0),
                (here & (z > 0), fw1b, 6, both, 0),
                (here & (z < last), bw1a, 12, both, 0),
                (here & (z < last), bw1b, 14, both, 0),
                (here & (z > 1), fw2a, 0, (1,), 0),
                (here & (z > 1), fw2b, 2, both, 0),
                (here & (z < last - 1), bw2a, 16, both, 0),
                (here & (z < last - 1), bw2b, 18, (0,), 0),
            ),
        )

    def work(late):
        square(late, 0, x_ref, y_ref, w_ref, None)

    for_half(z, z_count, work)


def stage_1(z_count, x_in, y_in, w_in, ends, cross, line, x_ref, y_ref, w_ref, sums, cubes, done):
    z = lax.axis_index("col")
    last = z_count - 1
    both = (0, 1)
    take_all(
        x_ref,
        w_ref,
        (
            (z == 0, ends, 6, both, 0),
            (z == last, ends, 12, both, 0),
            (z <= 1, cross, 2, both, 0),
            (z >= last - 1, cross, 16, both, 0),
            (z <= 1, line, 0, (1,), MIXED),
            (z >= last - 1, line, 18, (0,), 0),
        ),
    )

    def work(late):
        square(late, 1, x_ref, y_ref, w_ref, sums)
        purify(late, 1, x_ref, y_ref, w_ref, cubes, done)

    for_half(z, z_count, work)


def stage_2(z_count, x_in, y_in, w_in, sums, cubes, done, ends, x_ref, y_ref, w_ref, out, ready, sems):
    z = lax.axis_index("col")
    last = z_count - 1
    both = (0, 1)
    take_all(
        x_ref,
        w_ref,
        (
            (z == 0, ends, 4, both, 0),
            (z == last, ends, 14, both, 0),
        ),
    )

    def work(late):
        copies = []

        def send(i, early, offset, count):
            part = pl.ds(offset, count)
            copy = pltpu.make_async_copy(
                (done if early else ready).at[i, part], out.at[i, part], sems.at[i, early]
            )
            copy.start()
            copies.append(copy)

        square(late, 2, x_ref, y_ref, w_ref, sums)
        purify(late, 2, x_ref, y_ref, w_ref, cubes, ready, send)
        for copy in copies:
            copy.wait()

    for_half(z, z_count, work)


SMEM = pl.BlockSpec(memory_space=pltpu.SMEM)
VMEM = pl.BlockSpec(memory_space=pltpu.VMEM)
KEPT = [
    pltpu.VMEM((10, 2 * B, 16 * B), jnp.bfloat16),
    pltpu.VMEM((20 * B, 12 * B), jnp.bfloat16),
    pltpu.VMEM((20, 8, B), jnp.float32),
]
PARTIAL = [
    pltpu.VMEM((15, 2 * B, 2 * B), jnp.float32),
    pltpu.VMEM((10, 2 * B, 2 * B), jnp.float32),
    pltpu.VMEM((4, 8, B, B), jnp.bfloat16),
]


def call(kernel, z_count, outs, specs, aliases, scratch, flops, *operands):
    return pl.pallas_call(
        functools.partial(kernel, z_count),
        out_shape=outs,
        in_specs=[VMEM] * len(operands),
        out_specs=specs,
        input_output_aliases=aliases,
        scratch_shapes=scratch,
        compiler_params=pltpu.CompilerParams(vmem_limit_bytes=16 * 1024 * 1024),
        cost_estimate=pl.CostEstimate(flops=flops, bytes_accessed=10**6, transcendentals=0),
    )(*operands)


def compute(z_count, rows_0, rows_1, rows_2):
    kept = call(stage_0, z_count, KEPT, [VMEM] * 3, {}, [], 10**9, *rows_0)
    aliases = {0: 0, 1: 1, 2: 2}
    outs = KEPT + PARTIAL
    got = call(stage_1, z_count, outs, [VMEM] * 6, aliases, [], 6 * 10**9, *kept, *rows_1)
    outs = KEPT + [jax.ShapeDtypeStruct((4, 8, B, B), jnp.bfloat16)]
    specs = [VMEM] * 3 + [pl.BlockSpec(memory_space=pl.ANY)]
    scratch = [pltpu.VMEM((4, 8, B, B), jnp.bfloat16), pltpu.SemaphoreType.DMA((4, 2))]
    return call(stage_2, z_count, outs, specs, aliases, scratch, 6 * 10**9, *got, *rows_2)[3]


def copy_pairs(one, two, out_one, out_two):
    out_one[...] = one[...]
    out_two[...] = two[...]


PAIRS = [pltpu.VMEM((PAIR, B), jnp.bfloat16)] * 2


def packed(present, upper):
    return pl.pallas_call(
        pack,
        out_shape=PAIRS,
        in_specs=[SMEM, pl.BlockSpec(memory_space=pltpu.HBM)],
        out_specs=[VMEM, VMEM],
        scratch_shapes=[pltpu.VMEM(upper.shape, upper.dtype), pltpu.SemaphoreType.DMA((2,))],
        compiler_params=pltpu.CompilerParams(vmem_limit_bytes=56 * 1024 * 1024),
    )(present, upper)


def copied(pairs):
    return pl.pallas_call(
        copy_pairs,
        out_shape=PAIRS,
        in_specs=[VMEM, VMEM],
        out_specs=[VMEM, VMEM],
        compiler_params=pltpu.CompilerParams(vmem_limit_bytes=8 * 1024 * 1024),
    )(*pairs)


def per_device(upper, present):
    s_count, z_count = lax.axis_size("row"), lax.axis_size("col")
    z = lax.axis_index("col")
    last = z_count - 1

    def swap(block, odd, inner=False):
        pairs = [(i, i + 1) for i in range(odd, last, 2)]
        pairs += [(j, i) for i, j in pairs]
        pairs = [pair for pair in pairs if not (inner and pair[0] in (0, last))]
        return lax.ppermute(block, "col", pairs)

    def hop(block, route):
        pairs = [
            (i * z_count + a, (i + d) % s_count * z_count + b)
            for i in range(s_count)
            for a, d, b in route
        ]
        return lax.ppermute(block, ("row", "col"), pairs)

    own = packed(present, upper)
    again = copied(own)
    a1, b1 = swap(own[0], 0), swap(own[1], 1)
    a2, b2 = swap(again[1], 0), swap(again[0], 1)
    ra1, rb1 = swap(b1, 0, True), swap(a1, 1)
    ra2, rb2 = swap(b2, 0, True), swap(a2, 1)
    edge = (z == 0) | (z == last)
    if z_count == 4:
        to_end, beside = [(1, 1, 0), (2, -1, 3)], [(0, 1, 0), (1, 1, 1), (2, -1, 2), (3, -1, 3)]
        ends_first = hop(rb1, to_end)
        cross_first = hop(jnp.where(edge, ra1, rb1), beside)
        ends_last = hop(rb2, to_end)
        later = jnp.where(edge, ra2, rb2)
        cross_last = hop(jnp.where(z < 2, later[PAIR - ONE :], later[:ONE]), beside)
    else:
        route = [(last, 1, 0), (0, -1, last)]
        ends_first, ends_last = hop(own[0], route), hop(own[1], route)
        route = [(last - 1, 1, 0), (last, 1, 1), (0, -1, last - 1), (1, -1, last)]
        cross_first = hop(jnp.where(edge, own[0], own[1]), route)
        later = jnp.where(edge, own[1], own[0])
        cross_last = hop(jnp.where(z < 2, later[:ONE], later[PAIR - ONE :]), route)
    rows = (*own, a1, a2, b1, b2, ra1, ra2, rb1, rb2)
    return compute(z_count, rows, (ends_first, cross_first, cross_last), (ends_last,))


def solution(mesh):
    return jax.shard_map(
        per_device,
        mesh=mesh,
        in_specs=(P(("groups", "row", "col"), None, None, None), P(("groups", "row", "col"), None)),
        out_specs=P(("groups", "row", "col"), None, None, None),
        check_vma=False,
    )
```

```python
import functools

import jax
import jax.numpy as jnp
from jax import lax
from jax.experimental import pallas as pl
from jax.experimental.pallas import tpu as pltpu
from jax.sharding import PartitionSpec as P

B = 128
NT = (((1,), (1,)), ((), ()))
NN = (((1,), (0,)), ((), ()))

MIXED = 7 * B
TAIL = 8 * B
SECOND = 8 * B + 16
PAIR = 15 * B + 16
ONE = SECOND

LOW = {1: 1, 2: 1, 3: 1, 4: 2, 5: 2, 6: 1, 7: 1}
HIGH = {12: 1, 13: 1, 14: 2, 15: 2, 16: 1, 17: 1, 18: 1}


def blk(a, n=1):
    return pl.ds(a * B, n * B)


def x_stage(late, J, m):
    return max(late.get(min(2 * J, m), 0), late.get(min(2 * J + 1, m), 0))


def square_terms(late, J, L):
    return [
        (m, max(x_stage(late, J, m), x_stage(late, L, m))) for m in range(2 * L - 7, 2 * J + 9)
    ]


def y_stage(late, J, L):
    return max(stage for _, stage in square_terms(late, min(J, L), max(J, L)))


def cube_terms(late, I, L):
    return [
        (j, max(x_stage(late, I, j), y_stage(late, j // 2, L))) for j in range(2 * L - 7, 2 * I + 9)
    ]


def runs(columns):
    found = []
    for m in columns:
        if found and found[-1][0] + found[-1][1] == m:
            found[-1][1] += 1
        else:
            found.append([m, 1])
    return found


def triangles():
    p = lax.broadcasted_iota(jnp.int32, (B, B), 0)
    q = lax.broadcasted_iota(jnp.int32, (B, B), 1)
    return p, q


def pack(present_hbm, upper_hbm, one, two, present, upper, sems):
    p, q = triangles()
    right = lax.broadcasted_iota(jnp.int32, (1, B), 1) >= B // 2

    def block(r, k):
        w = present[r, k].astype(jnp.float32)
        return upper[r, k].astype(jnp.float32) * w

    odd = lax.rem(lax.axis_index("col"), 2)
    halves = (2 * odd, 2 - 2 * odd)
    pattern = pltpu.make_async_copy(present_hbm, present, sems.at[2])
    pattern.start()
    copies = []
    for n, first in enumerate(halves):
        part = pl.ds(first, 2)
        copies.append(pltpu.make_async_copy(upper_hbm.at[part], upper.at[part], sems.at[n]))
        copies[-1].start()
    pattern.wait()
    for first, out, copy in zip(halves, (one, two), copies):
        copy.wait()
        one, two = block(first, 0), block(first + 1, 0)
        out[pl.ds(MIXED, B)] = jnp.where(p <= q, one, two).astype(jnp.bfloat16)
        for r in range(2):
            for k in range(1, 8):
                out[pl.ds(SECOND * r + (k - 1) * B, B)] = block(first + r, k).astype(jnp.bfloat16)
        lines = [
            jnp.where(
                right,
                present[first + 1, k].astype(jnp.float32),
                present[first, k].astype(jnp.float32),
            )
            for k in range(8)
        ]
        lines.append(jnp.sum(jnp.where(p == q, two, 0.0), axis=0, keepdims=True))
        lines.append(jnp.zeros((7, B), jnp.float32))
        out[pl.ds(TAIL, 16)] = jnp.concatenate(lines, axis=0).astype(jnp.bfloat16)


def set_x(x_ref, a, b, value):
    x_ref[a // 2, blk(a % 2), blk(b - a // 2 * 2 + 7)] = value


def put(x_ref, w_ref, ref, a, rows=(0, 1), skip=0):
    p, q = triangles()
    mixed = ref[pl.ds(MIXED - skip, B)].astype(jnp.float32)
    turned = mixed.T
    tail = ref[pl.ds(TAIL - skip, 16)].astype(jnp.float32)
    for r in rows:
        w_ref[a + r] = jnp.broadcast_to(tail[:8, r * B // 2 : r * B // 2 + 1], (8, B))
        if r == 0:
            diagonal = jnp.where(p <= q, mixed, turned)
        else:
            diagonal = jnp.where(p > q, mixed, jnp.where(p < q, turned, tail[8:9]))
        set_x(x_ref, a + r, a + r, diagonal.astype(jnp.bfloat16))
        for k in range(1, 8):
            u = ref[pl.ds(SECOND * r - skip + (k - 1) * B, B)]
            set_x(x_ref, a + r, a + r + k, u)
            if k <= 18 - a - r:
                set_x(x_ref, a + r + k, a + r, u.T)


def square(late, now, x_ref, y_ref, w_ref, part_ref):
    zero = jnp.zeros((B, B), jnp.bfloat16)
    for L in range(4, 10):
        for J in range(L - 4, L + 1):
            terms = square_terms(late, J, L)
            end = max(stage for _, stage in terms)
            if now > end or (now == 0 and end > 0):
                continue
            mine = [m for m, stage in terms if (stage <= now if now < 2 else stage == 2)]
            s = None
            for m, n in runs(mine):
                t = lax.dot_general(
                    x_ref[J, :, blk(m - 2 * J + 7, n)],
                    x_ref[L, :, blk(m - 2 * L + 7, n)],
                    NT,
                    preferred_element_type=jnp.float32,
                )
                s = t if s is None else s + t
            place = L % 3 * 5 + J - L + 4
            if now < end:
                if s is not None:
                    part_ref[place] = s
                continue
            if now == 2 and len(mine) < len(terms):
                s = s + part_ref[place]
            for dj in range(2):
                for dl in range(2):
                    j, l = 2 * J + dj, 2 * L + dl
                    off = abs(l - j)
                    if off > 7 or j in (0, 19) or l in (0, 19):
                        y_ref[blk(j), blk(l - 8)] = zero
                    else:
                        w = w_ref[min(j, l), pl.ds(off, 1)]
                        y_ref[blk(j), blk(l - 8)] = (
                            s[dj * B : (dj + 1) * B, dl * B : (dl + 1) * B] * w
                        ).astype(jnp.bfloat16)


def purify(late, now, x_ref, y_ref, w_ref, part_ref, ready, send=None):
    for I in (4, 5):
        complete = {}
        for L in range(I, I + 5):
            terms = cube_terms(late, I, L)
            end = max(stage for _, stage in terms)
            mine = [j for j, stage in terms if (stage == 2) == (now == 2)]
            c = None
            for up in (True, False):
                for j, n in runs([j for j in mine if (j <= 2 * L) == up]):
                    left = x_ref[I, :, blk(j - 2 * I + 7, n)]
                    right = (
                        y_ref[blk(j, n), blk(2 * L - 8, 2)] if up else y_ref[blk(2 * L, 2), blk(j - 8, n)]
                    )
                    t = lax.dot_general(
                        left, right, NN if up else NT, preferred_element_type=jnp.float32
                    )
                    c = t if c is None else c + t
            place = (I - 4) * 5 + L - I
            if now < end:
                if c is not None:
                    part_ref[place] = c
                continue
            if now == 2 and end == 2 and len(mine) < len(terms):
                c = c + part_ref[place]
            for di in range(2):
                i = 2 * I + di
                offsets = [off for off in (2 * L - i, 2 * L + 1 - i) if 0 <= off <= 7]
                if not offsets:
                    continue
                for off in offsets:
                    if now == 2 and end < 2:
                        break
                    l = i + off
                    dl = l - 2 * L
                    w = w_ref[i, pl.ds(off, 1)]
                    sq = y_ref[blk(i), blk(l - 8)].astype(jnp.float32)
                    cube = w * c[di * B : (di + 1) * B, dl * B : (dl + 1) * B]
                    ready[i - 8, off] = (3.0 * sq - 2.0 * cube).astype(jnp.bfloat16)
                complete.setdefault((i - 8, end < 2), []).extend(offsets)
        if send is not None:
            for (i, early), offsets in complete.items():
                send(i, int(early), min(offsets), len(offsets))


def take_all(x_ref, w_ref, pieces):
    for here, ref, a, rows, skip in pieces:
        pl.when(here)(functools.partial(put, x_ref, w_ref, ref, a, rows, skip))


def for_half(z, z_count, work):
    low = z < z_count // 2
    pl.when(low)(functools.partial(work, LOW))
    pl.when(jnp.logical_not(low))(functools.partial(work, HIGH))


def stage_0(z_count, own1, own2, a1, a2, b1, b2, ra1, ra2, rb1, rb2, x_ref, y_ref, w_ref):
    zero = jnp.zeros((B, B), jnp.bfloat16)
    for c in range(16):
        set_x(x_ref, 0, c - 7, zero)
        set_x(x_ref, 19, c + 11, zero)
    for a in range(1, 19):
        set_x(x_ref, a, a + 8 if a % 2 == 0 else a - 8, zero)
    z = lax.axis_index("col")
    last = z_count - 1
    both = (0, 1)
    even = lax.rem(z, 2) == 0
    for here, (owna, ownb, fw1a, fw1b, bw1a, bw1b, fw2a, fw2b, bw2a, bw2b) in (
        (even, (own1, own2, b1, b2, a2, a1, rb1, rb2, ra2, ra1)),
        (jnp.logical_not(even), (own2, own1, a1, a2, b2, b1, ra1, ra2, rb2, rb1)),
    ):
        take_all(
            x_ref,
            w_ref,
            (
                (here, owna, 8, both, 0),
                (here, ownb, 10, both, 0),
                (here & (z > 0), fw1a, 4, both, 0),
                (here & (z > 0), fw1b, 6, both, 0),
                (here & (z < last), bw1a, 12, both, 0),
                (here & (z < last), bw1b, 14, both, 0),
                (here & (z > 1), fw2a, 0, (1,), 0),
                (here & (z > 1), fw2b, 2, both, 0),
                (here & (z < last - 1), bw2a, 16, both, 0),
                (here & (z < last - 1), bw2b, 18, (0,), 0),
            ),
        )

    def work(late):
        square(late, 0, x_ref, y_ref, w_ref, None)

    for_half(z, z_count, work)


def stage_1(z_count, x_in, y_in, w_in, ends, cross, line, x_ref, y_ref, w_ref, sums, cubes, done):
    z = lax.axis_index("col")
    last = z_count - 1
    both = (0, 1)
    take_all(
        x_ref,
        w_ref,
        (
            (z == 0, ends, 6, both, 0),
            (z == last, ends, 12, both, 0),
            (z <= 1, cross, 2, both, 0),
            (z >= last - 1, cross, 16, both, 0),
            (z <= 1, line, 0, (1,), MIXED),
            (z >= last - 1, line, 18, (0,), 0),
        ),
    )

    def work(late):
        square(late, 1, x_ref, y_ref, w_ref, sums)
        purify(late, 1, x_ref, y_ref, w_ref, cubes, done)

    for_half(z, z_count, work)


def stage_2(z_count, x_in, y_in, w_in, sums, cubes, done, ends, x_ref, y_ref, w_ref, out, ready, sems):
    z = lax.axis_index("col")
    last = z_count - 1
    both = (0, 1)
    take_all(
        x_ref,
        w_ref,
        (
            (z == 0, ends, 4, both, 0),
            (z == last, ends, 14, both, 0),
        ),
    )

    def work(late):
        copies = []

        def send(i, early, offset, count):
            part = pl.ds(offset, count)
            copy = pltpu.make_async_copy(
                (done if early else ready).at[i, part], out.at[i, part], sems.at[i, early]
            )
            copy.start()
            copies.append(copy)

        square(late, 2, x_ref, y_ref, w_ref, sums)
        purify(late, 2, x_ref, y_ref, w_ref, cubes, ready, send)
        for copy in copies:
            copy.wait()

    for_half(z, z_count, work)


SMEM = pl.BlockSpec(memory_space=pltpu.SMEM)
VMEM = pl.BlockSpec(memory_space=pltpu.VMEM)
KEPT = [
    pltpu.VMEM((10, 2 * B, 16 * B), jnp.bfloat16),
    pltpu.VMEM((20 * B, 12 * B), jnp.bfloat16),
    pltpu.VMEM((20, 8, B), jnp.float32),
]
PARTIAL = [
    pltpu.VMEM((15, 2 * B, 2 * B), jnp.float32),
    pltpu.VMEM((10, 2 * B, 2 * B), jnp.float32),
    pltpu.VMEM((4, 8, B, B), jnp.bfloat16),
]


def call(kernel, z_count, outs, specs, aliases, scratch, flops, *operands):
    return pl.pallas_call(
        functools.partial(kernel, z_count),
        out_shape=outs,
        in_specs=[VMEM] * len(operands),
        out_specs=specs,
        input_output_aliases=aliases,
        scratch_shapes=scratch,
        compiler_params=pltpu.CompilerParams(vmem_limit_bytes=16 * 1024 * 1024),
        cost_estimate=pl.CostEstimate(flops=flops, bytes_accessed=10**6, transcendentals=0),
    )(*operands)


def compute(z_count, rows_0, rows_1, rows_2):
    kept = call(stage_0, z_count, KEPT, [VMEM] * 3, {}, [], 10**9, *rows_0)
    aliases = {0: 0, 1: 1, 2: 2}
    outs = KEPT + PARTIAL
    got = call(stage_1, z_count, outs, [VMEM] * 6, aliases, [], 6 * 10**9, *kept, *rows_1)
    outs = KEPT + [jax.ShapeDtypeStruct((4, 8, B, B), jnp.bfloat16)]
    specs = [VMEM] * 3 + [pl.BlockSpec(memory_space=pl.ANY)]
    scratch = [pltpu.VMEM((4, 8, B, B), jnp.bfloat16), pltpu.SemaphoreType.DMA((4, 2))]
    return call(stage_2, z_count, outs, specs, aliases, scratch, 6 * 10**9, *got, *rows_2)[3]


def copy_pairs(one, two, out_one, out_two):
    out_one[...] = one[...]
    out_two[...] = two[...]


PAIRS = [pltpu.VMEM((PAIR, B), jnp.bfloat16)] * 2


def packed(present, upper):
    return pl.pallas_call(
        pack,
        out_shape=PAIRS,
        in_specs=[pl.BlockSpec(memory_space=pltpu.HBM)] * 2,
        out_specs=[VMEM, VMEM],
        scratch_shapes=[
            pltpu.SMEM(present.shape, present.dtype),
            pltpu.VMEM(upper.shape, upper.dtype),
            pltpu.SemaphoreType.DMA((3,)),
        ],
        compiler_params=pltpu.CompilerParams(vmem_limit_bytes=56 * 1024 * 1024),
    )(present, upper)


def copied(pairs):
    return pl.pallas_call(
        copy_pairs,
        out_shape=PAIRS,
        in_specs=[VMEM, VMEM],
        out_specs=[VMEM, VMEM],
        compiler_params=pltpu.CompilerParams(vmem_limit_bytes=8 * 1024 * 1024),
    )(*pairs)


def per_device(upper, present):
    s_count, z_count = lax.axis_size("row"), lax.axis_size("col")
    z = lax.axis_index("col")
    last = z_count - 1

    def swap(block, odd, inner=False):
        pairs = [(i, i + 1) for i in range(odd, last, 2)]
        pairs += [(j, i) for i, j in pairs]
        pairs = [pair for pair in pairs if not (inner and pair[0] in (0, last))]
        return lax.ppermute(block, "col", pairs)

    def hop(block, route):
        pairs = [
            (i * z_count + a, (i + d) % s_count * z_count + b)
            for i in range(s_count)
            for a, d, b in route
        ]
        return lax.ppermute(block, ("row", "col"), pairs)

    own = packed(present, upper)
    again = copied(own)
    a1, b1 = swap(own[0], 0), swap(own[1], 1)
    a2, b2 = swap(again[1], 0), swap(again[0], 1)
    ra1, rb1 = swap(b1, 0, True), swap(a1, 1)
    ra2, rb2 = swap(b2, 0, True), swap(a2, 1)
    edge = (z == 0) | (z == last)
    if z_count == 4:
        to_end, beside = [(1, 1, 0), (2, -1, 3)], [(0, 1, 0), (1, 1, 1), (2, -1, 2), (3, -1, 3)]
        ends_first = hop(rb1, to_end)
        cross_first = hop(jnp.where(edge, ra1, rb1), beside)
        ends_last = hop(rb2, to_end)
        later = jnp.where(edge, ra2, rb2)
        cross_last = hop(jnp.where(z < 2, later[PAIR - ONE :], later[:ONE]), beside)
    else:
        route = [(last, 1, 0), (0, -1, last)]
        ends_first, ends_last = hop(own[0], route), hop(own[1], route)
        route = [(last - 1, 1, 0), (last, 1, 1), (0, -1, last - 1), (1, -1, last)]
        cross_first = hop(jnp.where(edge, own[0], own[1]), route)
        later = jnp.where(edge, own[1], own[0])
        cross_last = hop(jnp.where(z < 2, later[:ONE], later[PAIR - ONE :]), route)
    rows = (*own, a1, a2, b1, b2, ra1, ra2, rb1, rb2)
    return compute(z_count, rows, (ends_first, cross_first, cross_last), (ends_last,))


def solution(mesh):
    return jax.shard_map(
        per_device,
        mesh=mesh,
        in_specs=(P(("groups", "row", "col"), None, None, None), P(("groups", "row", "col"), None)),
        out_specs=P(("groups", "row", "col"), None, None, None),
        check_vma=False,
    )
```

```python
import functools

import jax
import jax.numpy as jnp
from jax import lax
from jax.experimental import pallas as pl
from jax.experimental.pallas import tpu as pltpu
from jax.sharding import PartitionSpec as P

B = 128
NT = (((1,), (1,)), ((), ()))
NN = (((1,), (0,)), ((), ()))

MIXED = 7 * B
TAIL = 8 * B
SECOND = 8 * B + 16
PAIR = 15 * B + 16
ONE = SECOND

LOW = {1: 1, 2: 1, 3: 1, 4: 2, 5: 2, 6: 1, 7: 1}
HIGH = {12: 1, 13: 1, 14: 2, 15: 2, 16: 1, 17: 1, 18: 1}


def blk(a, n=1):
    return pl.ds(a * B, n * B)


def x_stage(late, J, m):
    return max(late.get(min(2 * J, m), 0), late.get(min(2 * J + 1, m), 0))


def square_terms(late, J, L):
    return [
        (m, max(x_stage(late, J, m), x_stage(late, L, m))) for m in range(2 * L - 7, 2 * J + 9)
    ]


def y_stage(late, J, L):
    return max(stage for _, stage in square_terms(late, min(J, L), max(J, L)))


def cube_terms(late, I, L):
    return [
        (j, max(x_stage(late, I, j), y_stage(late, j // 2, L))) for j in range(2 * L - 7, 2 * I + 9)
    ]


def runs(columns):
    found = []
    for m in columns:
        if found and found[-1][0] + found[-1][1] == m:
            found[-1][1] += 1
        else:
            found.append([m, 1])
    return found


def triangles():
    p = lax.broadcasted_iota(jnp.int32, (B, B), 0)
    q = lax.broadcasted_iota(jnp.int32, (B, B), 1)
    return p, q


def pack(present_hbm, upper_hbm, one, two, present, upper, sems):
    p, q = triangles()
    right = lax.broadcasted_iota(jnp.int32, (1, B), 1) >= B // 2

    def block(r, k):
        w = present[r, k].astype(jnp.float32)
        return upper[r, k].astype(jnp.float32) * w

    odd = lax.rem(lax.axis_index("col"), 2)
    halves = (2 * odd, 2 - 2 * odd)
    pattern = pltpu.make_async_copy(present_hbm, present, sems.at[2])
    pattern.start()
    copies = []
    for n, first in enumerate(halves):
        part = pl.ds(first, 2)
        copies.append(pltpu.make_async_copy(upper_hbm.at[part], upper.at[part], sems.at[n]))
        copies[-1].start()
    pattern.wait()
    for first, out, copy in zip(halves, (one, two), copies):
        copy.wait()
        one, two = block(first, 0), block(first + 1, 0)
        out[pl.ds(MIXED, B)] = jnp.where(p <= q, one, two).astype(jnp.bfloat16)
        for r in range(2):
            for k in range(1, 8):
                out[pl.ds(SECOND * r + (k - 1) * B, B)] = block(first + r, k).astype(jnp.bfloat16)
        lines = [
            jnp.where(
                right,
                present[first + 1, k].astype(jnp.float32),
                present[first, k].astype(jnp.float32),
            )
            for k in range(8)
        ]
        lines.append(jnp.sum(jnp.where(p == q, two, 0.0), axis=0, keepdims=True))
        lines.append(jnp.zeros((7, B), jnp.float32))
        out[pl.ds(TAIL, 16)] = jnp.concatenate(lines, axis=0).astype(jnp.bfloat16)


def set_x(x_ref, a, b, value):
    x_ref[a // 2, blk(a % 2), blk(b - a // 2 * 2 + 7)] = value


def put(x_ref, w_ref, ref, a, rows=(0, 1), skip=0):
    p, q = triangles()
    mixed = ref[pl.ds(MIXED - skip, B)].astype(jnp.float32)
    turned = mixed.T
    tail = ref[pl.ds(TAIL - skip, 16)].astype(jnp.float32)
    for r in rows:
        w_ref[a + r] = jnp.broadcast_to(tail[:8, r * B // 2 : r * B // 2 + 1], (8, B))
        if r == 0:
            diagonal = jnp.where(p <= q, mixed, turned)
        else:
            diagonal = jnp.where(p > q, mixed, jnp.where(p < q, turned, tail[8:9]))
        set_x(x_ref, a + r, a + r, diagonal.astype(jnp.bfloat16))
        for k in range(1, 8):
            u = ref[pl.ds(SECOND * r - skip + (k - 1) * B, B)]
            set_x(x_ref, a + r, a + r + k, u)
            if k <= 18 - a - r:
                set_x(x_ref, a + r + k, a + r, u.T)


def square(late, now, x_ref, y_ref, w_ref, part_ref):
    zero = jnp.zeros((B, B), jnp.bfloat16)
    for L in range(4, 10):
        for J in range(L - 4, L + 1):
            terms = square_terms(late, J, L)
            lo, size = (1, 1) if L - J == 4 else (0, 2)
            end = max(stage for _, stage in terms)
            if now > end or (now == 0 and end > 0):
                continue
            mine = [m for m, stage in terms if (stage <= now if now < 2 else stage == 2)]
            s = None
            for m, n in runs(mine):
                t = lax.dot_general(
                    x_ref[J, blk(lo, size), blk(m - 2 * J + 7, n)],
                    x_ref[L, blk(0, size), blk(m - 2 * L + 7, n)],
                    NT,
                    preferred_element_type=jnp.float32,
                )
                s = t if s is None else s + t
            place = L % 3 * 5 + J - L + 4
            if now < end:
                if s is not None:
                    part_ref[place, blk(0, size), blk(0, size)] = s
                continue
            if now == 2 and len(mine) < len(terms):
                s = s + part_ref[place, blk(0, size), blk(0, size)]
            for dj in range(2):
                for dl in range(2):
                    j, l = 2 * J + dj, 2 * L + dl
                    off = abs(l - j)
                    if off > 7 or j in (0, 19) or l in (0, 19):
                        y_ref[blk(j), blk(l - 8)] = zero
                    else:
                        w = w_ref[min(j, l), pl.ds(off, 1)]
                        y_ref[blk(j), blk(l - 8)] = (
                            s[(dj - lo) * B : (dj - lo + 1) * B, dl * B : (dl + 1) * B] * w
                        ).astype(jnp.bfloat16)


def purify(late, now, x_ref, y_ref, w_ref, part_ref, ready, send=None):
    for I in (4, 5):
        complete = {}
        for L in range(I, I + 5):
            terms = cube_terms(late, I, L)
            lo, size = (1, 1) if L - I == 4 else (0, 2)
            end = max(stage for _, stage in terms)
            mine = [j for j, stage in terms if (stage == 2) == (now == 2)]
            c = None
            for up in (True, False):
                for j, n in runs([j for j in mine if (j <= 2 * L) == up]):
                    left = x_ref[I, blk(lo, size), blk(j - 2 * I + 7, n)]
                    right = (
                        y_ref[blk(j, n), blk(2 * L - 8, size)]
                        if up
                        else y_ref[blk(2 * L, size), blk(j - 8, n)]
                    )
                    t = lax.dot_general(
                        left, right, NN if up else NT, preferred_element_type=jnp.float32
                    )
                    c = t if c is None else c + t
            place = (I - 4) * 5 + L - I
            if now < end:
                if c is not None:
                    part_ref[place, blk(0, size), blk(0, size)] = c
                continue
            if now == 2 and end == 2 and len(mine) < len(terms):
                c = c + part_ref[place, blk(0, size), blk(0, size)]
            for di in range(2):
                i = 2 * I + di
                offsets = [off for off in (2 * L - i, 2 * L + 1 - i) if 0 <= off <= 7]
                if not offsets:
                    continue
                for off in offsets:
                    if now == 2 and end < 2:
                        break
                    l = i + off
                    dl = l - 2 * L
                    w = w_ref[i, pl.ds(off, 1)]
                    sq = y_ref[blk(i), blk(l - 8)].astype(jnp.float32)
                    cube = w * c[(di - lo) * B : (di - lo + 1) * B, dl * B : (dl + 1) * B]
                    ready[i - 8, off] = (3.0 * sq - 2.0 * cube).astype(jnp.bfloat16)
                complete.setdefault((i - 8, end < 2), []).extend(offsets)
        if send is not None:
            for (i, early), offsets in complete.items():
                send(i, int(early), min(offsets), len(offsets))


def take_all(x_ref, w_ref, pieces):
    for here, ref, a, rows, skip in pieces:
        pl.when(here)(functools.partial(put, x_ref, w_ref, ref, a, rows, skip))


def for_half(z, z_count, work):
    low = z < z_count // 2
    pl.when(low)(functools.partial(work, LOW))
    pl.when(jnp.logical_not(low))(functools.partial(work, HIGH))


def stage_0(z_count, own1, own2, a1, a2, b1, b2, ra1, ra2, rb1, rb2, x_ref, y_ref, w_ref):
    zero = jnp.zeros((B, B), jnp.bfloat16)
    for c in range(16):
        set_x(x_ref, 0, c - 7, zero)
        set_x(x_ref, 19, c + 11, zero)
    for a in range(1, 19):
        set_x(x_ref, a, a + 8 if a % 2 == 0 else a - 8, zero)
    z = lax.axis_index("col")
    last = z_count - 1
    both = (0, 1)
    even = lax.rem(z, 2) == 0
    for here, (owna, ownb, fw1a, fw1b, bw1a, bw1b, fw2a, fw2b, bw2a, bw2b) in (
        (even, (own1, own2, b1, b2, a2, a1, rb1, rb2, ra2, ra1)),
        (jnp.logical_not(even), (own2, own1, a1, a2, b2, b1, ra1, ra2, rb2, rb1)),
    ):
        take_all(
            x_ref,
            w_ref,
            (
                (here, owna, 8, both, 0),
                (here, ownb, 10, both, 0),
                (here & (z > 0), fw1a, 4, both, 0),
                (here & (z > 0), fw1b, 6, both, 0),
                (here & (z < last), bw1a, 12, both, 0),
                (here & (z < last), bw1b, 14, both, 0),
                (here & (z > 1), fw2a, 0, (1,), 0),
                (here & (z > 1), fw2b, 2, both, 0),
                (here & (z < last - 1), bw2a, 16, both, 0),
                (here & (z < last - 1), bw2b, 18, (0,), 0),
            ),
        )

    def work(late):
        square(late, 0, x_ref, y_ref, w_ref, None)

    for_half(z, z_count, work)


def stage_1(z_count, x_in, y_in, w_in, ends, cross, line, x_ref, y_ref, w_ref, sums, cubes, done):
    z = lax.axis_index("col")
    last = z_count - 1
    both = (0, 1)
    take_all(
        x_ref,
        w_ref,
        (
            (z == 0, ends, 6, both, 0),
            (z == last, ends, 12, both, 0),
            (z <= 1, cross, 2, both, 0),
            (z >= last - 1, cross, 16, both, 0),
            (z <= 1, line, 0, (1,), MIXED),
            (z >= last - 1, line, 18, (0,), 0),
        ),
    )

    def work(late):
        square(late, 1, x_ref, y_ref, w_ref, sums)
        purify(late, 1, x_ref, y_ref, w_ref, cubes, done)

    for_half(z, z_count, work)


def stage_2(z_count, x_in, y_in, w_in, sums, cubes, done, ends, x_ref, y_ref, w_ref, out, ready, sems):
    z = lax.axis_index("col")
    last = z_count - 1
    both = (0, 1)
    take_all(
        x_ref,
        w_ref,
        (
            (z == 0, ends, 4, both, 0),
            (z == last, ends, 14, both, 0),
        ),
    )

    def work(late):
        copies = []

        def send(i, early, offset, count):
            part = pl.ds(offset, count)
            copy = pltpu.make_async_copy(
                (done if early else ready).at[i, part], out.at[i, part], sems.at[i, early]
            )
            copy.start()
            copies.append(copy)

        square(late, 2, x_ref, y_ref, w_ref, sums)
        purify(late, 2, x_ref, y_ref, w_ref, cubes, ready, send)
        for copy in copies:
            copy.wait()

    for_half(z, z_count, work)


SMEM = pl.BlockSpec(memory_space=pltpu.SMEM)
VMEM = pl.BlockSpec(memory_space=pltpu.VMEM)
KEPT = [
    pltpu.VMEM((10, 2 * B, 16 * B), jnp.bfloat16),
    pltpu.VMEM((20 * B, 12 * B), jnp.bfloat16),
    pltpu.VMEM((20, 8, B), jnp.float32),
]
PARTIAL = [
    pltpu.VMEM((15, 2 * B, 2 * B), jnp.float32),
    pltpu.VMEM((10, 2 * B, 2 * B), jnp.float32),
    pltpu.VMEM((4, 8, B, B), jnp.bfloat16),
]


def call(kernel, z_count, outs, specs, aliases, scratch, flops, *operands):
    return pl.pallas_call(
        functools.partial(kernel, z_count),
        out_shape=outs,
        in_specs=[VMEM] * len(operands),
        out_specs=specs,
        input_output_aliases=aliases,
        scratch_shapes=scratch,
        compiler_params=pltpu.CompilerParams(vmem_limit_bytes=16 * 1024 * 1024),
        cost_estimate=pl.CostEstimate(flops=flops, bytes_accessed=10**6, transcendentals=0),
    )(*operands)


def compute(z_count, rows_0, rows_1, rows_2):
    kept = call(stage_0, z_count, KEPT, [VMEM] * 3, {}, [], 10**9, *rows_0)
    aliases = {0: 0, 1: 1, 2: 2}
    outs = KEPT + PARTIAL
    got = call(stage_1, z_count, outs, [VMEM] * 6, aliases, [], 6 * 10**9, *kept, *rows_1)
    outs = KEPT + [jax.ShapeDtypeStruct((4, 8, B, B), jnp.bfloat16)]
    specs = [VMEM] * 3 + [pl.BlockSpec(memory_space=pl.ANY)]
    scratch = [pltpu.VMEM((4, 8, B, B), jnp.bfloat16), pltpu.SemaphoreType.DMA((4, 2))]
    return call(stage_2, z_count, outs, specs, aliases, scratch, 6 * 10**9, *got, *rows_2)[3]


def copy_pairs(one, two, out_one, out_two):
    out_one[...] = one[...]
    out_two[...] = two[...]


PAIRS = [pltpu.VMEM((PAIR, B), jnp.bfloat16)] * 2


def packed(present, upper):
    return pl.pallas_call(
        pack,
        out_shape=PAIRS,
        in_specs=[pl.BlockSpec(memory_space=pltpu.HBM)] * 2,
        out_specs=[VMEM, VMEM],
        scratch_shapes=[
            pltpu.SMEM(present.shape, present.dtype),
            pltpu.VMEM(upper.shape, upper.dtype),
            pltpu.SemaphoreType.DMA((3,)),
        ],
        compiler_params=pltpu.CompilerParams(vmem_limit_bytes=56 * 1024 * 1024),
    )(present, upper)


def copied(pairs):
    return pl.pallas_call(
        copy_pairs,
        out_shape=PAIRS,
        in_specs=[VMEM, VMEM],
        out_specs=[VMEM, VMEM],
        compiler_params=pltpu.CompilerParams(vmem_limit_bytes=8 * 1024 * 1024),
    )(*pairs)


def per_device(upper, present):
    s_count, z_count = lax.axis_size("row"), lax.axis_size("col")
    z = lax.axis_index("col")
    last = z_count - 1

    def swap(block, odd, inner=False):
        pairs = [(i, i + 1) for i in range(odd, last, 2)]
        pairs += [(j, i) for i, j in pairs]
        pairs = [pair for pair in pairs if not (inner and pair[0] in (0, last))]
        return lax.ppermute(block, "col", pairs)

    def hop(block, route):
        pairs = [
            (i * z_count + a, (i + d) % s_count * z_count + b)
            for i in range(s_count)
            for a, d, b in route
        ]
        return lax.ppermute(block, ("row", "col"), pairs)

    own = packed(present, upper)
    again = copied(own)
    a1, b1 = swap(own[0], 0), swap(own[1], 1)
    a2, b2 = swap(again[1], 0), swap(again[0], 1)
    ra1, rb1 = swap(b1, 0, True), swap(a1, 1)
    ra2, rb2 = swap(b2, 0, True), swap(a2, 1)
    edge = (z == 0) | (z == last)
    if z_count == 4:
        to_end, beside = [(1, 1, 0), (2, -1, 3)], [(0, 1, 0), (1, 1, 1), (2, -1, 2), (3, -1, 3)]
        ends_first = hop(rb1, to_end)
        cross_first = hop(jnp.where(edge, ra1, rb1), beside)
        ends_last = hop(rb2, to_end)
        later = jnp.where(edge, ra2, rb2)
        cross_last = hop(jnp.where(z < 2, later[PAIR - ONE :], later[:ONE]), beside)
    else:
        route = [(last, 1, 0), (0, -1, last)]
        ends_first, ends_last = hop(own[0], route), hop(own[1], route)
        route = [(last - 1, 1, 0), (last, 1, 1), (0, -1, last - 1), (1, -1, last)]
        cross_first = hop(jnp.where(edge, own[0], own[1]), route)
        later = jnp.where(edge, own[1], own[0])
        cross_last = hop(jnp.where(z < 2, later[:ONE], later[PAIR - ONE :]), route)
    rows = (*own, a1, a2, b1, b2, ra1, ra2, rb1, rb2)
    return compute(z_count, rows, (ends_first, cross_first, cross_last), (ends_last,))


def solution(mesh):
    return jax.shard_map(
        per_device,
        mesh=mesh,
        in_specs=(P(("groups", "row", "col"), None, None, None), P(("groups", "row", "col"), None)),
        out_specs=P(("groups", "row", "col"), None, None, None),
        check_vma=False,
    )
```

```python
import functools

import jax
import jax.numpy as jnp
from jax import lax
from jax.experimental import pallas as pl
from jax.experimental.pallas import tpu as pltpu
from jax.sharding import PartitionSpec as P

B = 128
NT = (((1,), (1,)), ((), ()))
NN = (((1,), (0,)), ((), ()))

MIXED = 7 * B
TAIL = 8 * B
SECOND = 8 * B + 16
PAIR = 15 * B + 16
ONE = SECOND

LOW = {1: 1, 2: 1, 3: 1, 4: 2, 5: 2, 6: 1, 7: 1}
HIGH = {12: 1, 13: 1, 14: 2, 15: 2, 16: 1, 17: 1, 18: 1}


def blk(a, n=1):
    return pl.ds(a * B, n * B)


def x_stage(late, J, m):
    return max(late.get(min(2 * J, m), 0), late.get(min(2 * J + 1, m), 0))


def square_terms(late, J, L):
    return [
        (m, max(x_stage(late, J, m), x_stage(late, L, m))) for m in range(2 * L - 7, 2 * J + 9)
    ]


def y_stage(late, J, L):
    return max(stage for _, stage in square_terms(late, min(J, L), max(J, L)))


def cube_terms(late, I, L):
    return [
        (j, max(x_stage(late, I, j), y_stage(late, j // 2, L))) for j in range(2 * L - 7, 2 * I + 9)
    ]


def runs(columns):
    found = []
    for m in columns:
        if found and found[-1][0] + found[-1][1] == m:
            found[-1][1] += 1
        else:
            found.append([m, 1])
    return found


def triangles():
    p = lax.broadcasted_iota(jnp.int32, (B, B), 0)
    q = lax.broadcasted_iota(jnp.int32, (B, B), 1)
    return p, q


def pack(present_hbm, upper_hbm, one, two, present, upper, sems):
    p, q = triangles()
    right = lax.broadcasted_iota(jnp.int32, (1, B), 1) >= B // 2

    def block(r, k):
        w = present[r, k].astype(jnp.float32)
        return upper[r, k].astype(jnp.float32) * w

    odd = lax.rem(lax.axis_index("col"), 2)
    halves = (2 * odd, 2 - 2 * odd)
    pattern = pltpu.make_async_copy(present_hbm, present, sems.at[2])
    pattern.start()
    copies = []
    for n, first in enumerate(halves):
        part = pl.ds(first, 2)
        copies.append(pltpu.make_async_copy(upper_hbm.at[part], upper.at[part], sems.at[n]))
        copies[-1].start()
    pattern.wait()
    for first, out, copy in zip(halves, (one, two), copies):
        copy.wait()
        one, two = block(first, 0), block(first + 1, 0)
        out[pl.ds(MIXED, B)] = jnp.where(p <= q, one, two).astype(jnp.bfloat16)
        for r in range(2):
            for k in range(1, 8):
                out[pl.ds(SECOND * r + (k - 1) * B, B)] = block(first + r, k).astype(jnp.bfloat16)
        lines = [
            jnp.where(
                right,
                present[first + 1, k].astype(jnp.float32),
                present[first, k].astype(jnp.float32),
            )
            for k in range(8)
        ]
        lines.append(jnp.sum(jnp.where(p == q, two, 0.0), axis=0, keepdims=True))
        lines.append(jnp.zeros((7, B), jnp.float32))
        out[pl.ds(TAIL, 16)] = jnp.concatenate(lines, axis=0).astype(jnp.bfloat16)


def set_x(x_ref, a, b, value):
    x_ref[a // 2, blk(a % 2), blk(b - a // 2 * 2 + 7)] = value


def put(x_ref, w_ref, ref, a, rows=(0, 1), skip=0):
    p, q = triangles()
    mixed = ref[pl.ds(MIXED - skip, B)].astype(jnp.float32)
    turned = mixed.T
    tail = ref[pl.ds(TAIL - skip, 16)].astype(jnp.float32)
    for r in rows:
        w_ref[a + r] = jnp.broadcast_to(tail[:8, r * B // 2 : r * B // 2 + 1], (8, B))
        if r == 0:
            diagonal = jnp.where(p <= q, mixed, turned)
        else:
            diagonal = jnp.where(p > q, mixed, jnp.where(p < q, turned, tail[8:9]))
        set_x(x_ref, a + r, a + r, diagonal.astype(jnp.bfloat16))
        for k in range(1, 8):
            u = ref[pl.ds(SECOND * r - skip + (k - 1) * B, B)]
            set_x(x_ref, a + r, a + r + k, u)
            if k <= 18 - a - r:
                set_x(x_ref, a + r + k, a + r, u.T)


def square(late, now, x_ref, y_ref, w_ref, part_ref):
    zero = jnp.zeros((B, B), jnp.bfloat16)
    for L in range(4, 10):
        for J in range(L - 4, L + 1):
            terms = square_terms(late, J, L)
            lo, size = (1, 1) if L - J == 4 else (0, 2)
            end = max(stage for _, stage in terms)
            if now > end or (now == 0 and end > 0):
                continue
            mine = [m for m, stage in terms if (stage <= now if now < 2 else stage == 2)]
            s = None
            for m, n in runs(mine):
                t = lax.dot_general(
                    x_ref[J, blk(lo, size), blk(m - 2 * J + 7, n)],
                    x_ref[L, blk(0, size), blk(m - 2 * L + 7, n)],
                    NT,
                    preferred_element_type=jnp.float32,
                )
                s = t if s is None else s + t
            place = L % 3 * 5 + J - L + 4
            if now < end:
                if s is not None:
                    part_ref[place, blk(0, size), blk(0, size)] = s
                continue
            if now == 2 and len(mine) < len(terms):
                s = s + part_ref[place, blk(0, size), blk(0, size)]
            for dj in range(2):
                for dl in range(2):
                    j, l = 2 * J + dj, 2 * L + dl
                    off = abs(l - j)
                    if off > 7 or j in (0, 19) or l in (0, 19):
                        y_ref[blk(j), blk(l - 8)] = zero
                    else:
                        w = w_ref[min(j, l), pl.ds(off, 1)]
                        y_ref[blk(j), blk(l - 8)] = (
                            s[(dj - lo) * B : (dj - lo + 1) * B, dl * B : (dl + 1) * B] * w
                        ).astype(jnp.bfloat16)


def before(late, i):
    pairs = [(L, max(stage for _, stage in cube_terms(late, i // 2, L))) for L in range(i // 2, i // 2 + 5)]
    return [l - i for L, end in pairs if end < 2 for l in (2 * L, 2 * L + 1) if 0 <= l - i <= 7]


def purify(late, now, x_ref, y_ref, w_ref, part_ref, ready, send=None):
    for I in (4, 5):
        complete = {}
        for L in range(I, I + 5):
            terms = cube_terms(late, I, L)
            lo, size = (1, 1) if L - I == 4 else (0, 2)
            end = max(stage for _, stage in terms)
            mine = [j for j, stage in terms if (stage == 2) == (now == 2)]
            c = None
            for up in (True, False):
                for j, n in runs([j for j in mine if (j <= 2 * L) == up]):
                    left = x_ref[I, blk(lo, size), blk(j - 2 * I + 7, n)]
                    right = (
                        y_ref[blk(j, n), blk(2 * L - 8, size)]
                        if up
                        else y_ref[blk(2 * L, size), blk(j - 8, n)]
                    )
                    t = lax.dot_general(
                        left, right, NN if up else NT, preferred_element_type=jnp.float32
                    )
                    c = t if c is None else c + t
            place = (I - 4) * 5 + L - I
            if now < end:
                if c is not None:
                    part_ref[place, blk(0, size), blk(0, size)] = c
                continue
            if now == 2 and end == 2 and len(mine) < len(terms):
                c = c + part_ref[place, blk(0, size), blk(0, size)]
            for di in range(2):
                i = 2 * I + di
                offsets = [off for off in (2 * L - i, 2 * L + 1 - i) if 0 <= off <= 7]
                if not offsets or (now == 2 and end < 2):
                    continue
                for off in offsets:
                    l = i + off
                    dl = l - 2 * L
                    w = w_ref[i, pl.ds(off, 1)]
                    sq = y_ref[blk(i), blk(l - 8)].astype(jnp.float32)
                    cube = w * c[(di - lo) * B : (di - lo + 1) * B, dl * B : (dl + 1) * B]
                    ready[i - 8, off] = (3.0 * sq - 2.0 * cube).astype(jnp.bfloat16)
                complete.setdefault(i - 8, []).extend(offsets)
            if send is not None and L in (I + 2, I + 4):
                for i, offsets in complete.items():
                    send(i, int(L > I + 2), min(offsets), len(offsets))
                complete = {}


def take_all(x_ref, w_ref, pieces):
    for here, ref, a, rows, skip in pieces:
        pl.when(here)(functools.partial(put, x_ref, w_ref, ref, a, rows, skip))


def for_half(z, z_count, work):
    low = z < z_count // 2
    pl.when(low)(functools.partial(work, LOW))
    pl.when(jnp.logical_not(low))(functools.partial(work, HIGH))


def stage_0(z_count, own1, own2, a1, a2, b1, b2, ra1, ra2, rb1, rb2, x_ref, y_ref, w_ref):
    zero = jnp.zeros((B, B), jnp.bfloat16)
    for c in range(16):
        set_x(x_ref, 0, c - 7, zero)
        set_x(x_ref, 19, c + 11, zero)
    for a in range(1, 19):
        set_x(x_ref, a, a + 8 if a % 2 == 0 else a - 8, zero)
    z = lax.axis_index("col")
    last = z_count - 1
    both = (0, 1)
    even = lax.rem(z, 2) == 0
    for here, (owna, ownb, fw1a, fw1b, bw1a, bw1b, fw2a, fw2b, bw2a, bw2b) in (
        (even, (own1, own2, b1, b2, a2, a1, rb1, rb2, ra2, ra1)),
        (jnp.logical_not(even), (own2, own1, a1, a2, b2, b1, ra1, ra2, rb2, rb1)),
    ):
        take_all(
            x_ref,
            w_ref,
            (
                (here, owna, 8, both, 0),
                (here, ownb, 10, both, 0),
                (here & (z > 0), fw1a, 4, both, 0),
                (here & (z > 0), fw1b, 6, both, 0),
                (here & (z < last), bw1a, 12, both, 0),
                (here & (z < last), bw1b, 14, both, 0),
                (here & (z > 1), fw2a, 0, (1,), 0),
                (here & (z > 1), fw2b, 2, both, 0),
                (here & (z < last - 1), bw2a, 16, both, 0),
                (here & (z < last - 1), bw2b, 18, (0,), 0),
            ),
        )

    def work(late):
        square(late, 0, x_ref, y_ref, w_ref, None)

    for_half(z, z_count, work)


def stage_1(z_count, x_in, y_in, w_in, ends, cross, line, x_ref, y_ref, w_ref, sums, cubes, done):
    z = lax.axis_index("col")
    last = z_count - 1
    both = (0, 1)
    take_all(
        x_ref,
        w_ref,
        (
            (z == 0, ends, 6, both, 0),
            (z == last, ends, 12, both, 0),
            (z <= 1, cross, 2, both, 0),
            (z >= last - 1, cross, 16, both, 0),
            (z <= 1, line, 0, (1,), MIXED),
            (z >= last - 1, line, 18, (0,), 0),
        ),
    )

    def work(late):
        square(late, 1, x_ref, y_ref, w_ref, sums)
        purify(late, 1, x_ref, y_ref, w_ref, cubes, done)

    for_half(z, z_count, work)


def stage_2(z_count, x_in, y_in, w_in, sums, cubes, done, ends, x_ref, y_ref, w_ref, out, ready, sems):
    z = lax.axis_index("col")
    last = z_count - 1
    both = (0, 1)
    take_all(
        x_ref,
        w_ref,
        (
            (z == 0, ends, 4, both, 0),
            (z == last, ends, 14, both, 0),
        ),
    )

    def work(late):
        copies = []

        def send(i, turn, offset, count):
            part = pl.ds(offset, count)
            copy = pltpu.make_async_copy(
                (done if turn == 2 else ready).at[i, part], out.at[i, part], sems.at[i, turn]
            )
            copy.start()
            copies.append(copy)

        for i in range(4):
            offsets = before(late, i + 8)
            if offsets:
                send(i, 2, min(offsets), len(offsets))
        square(late, 2, x_ref, y_ref, w_ref, sums)
        purify(late, 2, x_ref, y_ref, w_ref, cubes, ready, send)
        for copy in copies:
            copy.wait()

    for_half(z, z_count, work)


SMEM = pl.BlockSpec(memory_space=pltpu.SMEM)
VMEM = pl.BlockSpec(memory_space=pltpu.VMEM)
KEPT = [
    pltpu.VMEM((10, 2 * B, 16 * B), jnp.bfloat16),
    pltpu.VMEM((20 * B, 12 * B), jnp.bfloat16),
    pltpu.VMEM((20, 8, B), jnp.float32),
]
PARTIAL = [
    pltpu.VMEM((15, 2 * B, 2 * B), jnp.float32),
    pltpu.VMEM((10, 2 * B, 2 * B), jnp.float32),
    pltpu.VMEM((4, 8, B, B), jnp.bfloat16),
]


def call(kernel, z_count, outs, specs, aliases, scratch, flops, *operands):
    return pl.pallas_call(
        functools.partial(kernel, z_count),
        out_shape=outs,
        in_specs=[VMEM] * len(operands),
        out_specs=specs,
        input_output_aliases=aliases,
        scratch_shapes=scratch,
        compiler_params=pltpu.CompilerParams(vmem_limit_bytes=16 * 1024 * 1024),
        cost_estimate=pl.CostEstimate(flops=flops, bytes_accessed=10**6, transcendentals=0),
    )(*operands)


def compute(z_count, rows_0, rows_1, rows_2):
    kept = call(stage_0, z_count, KEPT, [VMEM] * 3, {}, [], 10**9, *rows_0)
    aliases = {0: 0, 1: 1, 2: 2}
    outs = KEPT + PARTIAL
    got = call(stage_1, z_count, outs, [VMEM] * 6, aliases, [], 6 * 10**9, *kept, *rows_1)
    outs = KEPT + [jax.ShapeDtypeStruct((4, 8, B, B), jnp.bfloat16)]
    specs = [VMEM] * 3 + [pl.BlockSpec(memory_space=pl.ANY)]
    scratch = [pltpu.VMEM((4, 8, B, B), jnp.bfloat16), pltpu.SemaphoreType.DMA((4, 3))]
    return call(stage_2, z_count, outs, specs, aliases, scratch, 6 * 10**9, *got, *rows_2)[3]


def copy_pairs(one, two, out_one, out_two):
    out_one[...] = one[...]
    out_two[...] = two[...]


PAIRS = [pltpu.VMEM((PAIR, B), jnp.bfloat16)] * 2


def packed(present, upper):
    return pl.pallas_call(
        pack,
        out_shape=PAIRS,
        in_specs=[pl.BlockSpec(memory_space=pltpu.HBM)] * 2,
        out_specs=[VMEM, VMEM],
        scratch_shapes=[
            pltpu.SMEM(present.shape, present.dtype),
            pltpu.VMEM(upper.shape, upper.dtype),
            pltpu.SemaphoreType.DMA((3,)),
        ],
        compiler_params=pltpu.CompilerParams(vmem_limit_bytes=56 * 1024 * 1024),
    )(present, upper)


def copied(pairs):
    return pl.pallas_call(
        copy_pairs,
        out_shape=PAIRS,
        in_specs=[VMEM, VMEM],
        out_specs=[VMEM, VMEM],
        compiler_params=pltpu.CompilerParams(vmem_limit_bytes=8 * 1024 * 1024),
    )(*pairs)


def per_device(upper, present):
    s_count, z_count = lax.axis_size("row"), lax.axis_size("col")
    z = lax.axis_index("col")
    last = z_count - 1

    def swap(block, odd, inner=False):
        pairs = [(i, i + 1) for i in range(odd, last, 2)]
        pairs += [(j, i) for i, j in pairs]
        pairs = [pair for pair in pairs if not (inner and pair[0] in (0, last))]
        return lax.ppermute(block, "col", pairs)

    def hop(block, route):
        pairs = [
            (i * z_count + a, (i + d) % s_count * z_count + b)
            for i in range(s_count)
            for a, d, b in route
        ]
        return lax.ppermute(block, ("row", "col"), pairs)

    own = packed(present, upper)
    again = copied(own)
    a1, b1 = swap(own[0], 0), swap(own[1], 1)
    a2, b2 = swap(again[1], 0), swap(again[0], 1)
    ra1, rb1 = swap(b1, 0, True), swap(a1, 1)
    ra2, rb2 = swap(b2, 0, True), swap(a2, 1)
    edge = (z == 0) | (z == last)
    if z_count == 4:
        to_end, beside = [(1, 1, 0), (2, -1, 3)], [(0, 1, 0), (1, 1, 1), (2, -1, 2), (3, -1, 3)]
        ends_first = hop(rb1, to_end)
        cross_first = hop(jnp.where(edge, ra1, rb1), beside)
        ends_last = hop(rb2, to_end)
        later = jnp.where(edge, ra2, rb2)
        cross_last = hop(jnp.where(z < 2, later[PAIR - ONE :], later[:ONE]), beside)
    else:
        route = [(last, 1, 0), (0, -1, last)]
        ends_first, ends_last = hop(own[0], route), hop(own[1], route)
        route = [(last - 1, 1, 0), (last, 1, 1), (0, -1, last - 1), (1, -1, last)]
        cross_first = hop(jnp.where(edge, own[0], own[1]), route)
        later = jnp.where(edge, own[1], own[0])
        cross_last = hop(jnp.where(z < 2, later[:ONE], later[PAIR - ONE :]), route)
    rows = (*own, a1, a2, b1, b2, ra1, ra2, rb1, rb2)
    return compute(z_count, rows, (ends_first, cross_first, cross_last), (ends_last,))


def solution(mesh):
    return jax.shard_map(
        per_device,
        mesh=mesh,
        in_specs=(P(("groups", "row", "col"), None, None, None), P(("groups", "row", "col"), None)),
        out_specs=P(("groups", "row", "col"), None, None, None),
        check_vma=False,
    )
```
